256 devices in a mesh: pts: 32 (over y, x, core), bas: 8 (over z).
Axes of the slice: x: 4, y: 4, z: 8, core: 2. Of those that a mesh axis runs over, the one named last changes fastest.
Arguments:
- chi: bfloat16 [128, 448, 2048], P('pts'), may hold values from -6 to 6
- dchi: bfloat16 [3, 128, 448, 2048], P(None, 'pts', None, 'bas'), may hold values from -6 to 6
- screen: int32 [128, 16], P('pts'), may hold values from 0 to 127, as said below
- density: bfloat16 [128, 128, 128, 128], P('pts', 'bas'), may hold values from -0.125 to 0.125
- weights: float32 [128, 448], P('pts'), may hold values from 0.002 to 0.02
- basis_atom: int32 [16384], P('bas'), may hold values from 0 to 3071, never falling along the last dimension, each value on 1 to 14 neighbouring positions
- neighbors: int32 [8, 57344], P(None, ('pts', 'bas')), may hold values from 0 to 3071
- weight_grad: float32 [3, 8, 57344], P(None, None, ('pts', 'bas')), may hold values from -0.046875 to 0.046875
Outputs:
- gradient: float32 [3, 3072], P(None, ('pts', 'bas'))
The draws below stay inside these ranges and needn't reach their ends.
Inputs may be any that keep to these rules, and one draw needn't show every extreme that they name: `screen`: slot j of a box names a basis block k with k // 16 == j // 2. For a box on index q of pts, the slots with j // 2 == q // 4 name distinct blocks with k // 4 == q, and every other slot names a block with k // 4 != q. Among the 64 slots of the boxes of one index of pts, at most 8 name blocks with one value of k // 4, and at most 4 name blocks with one value of k // 4 other than that index.
All inputs are finite; a program needn't handle non-finite values.
Results may differ from the reference program's by a relative error of at most 0.0003.
Values may be sent and summed in bfloat16 or wider, within the bound.
No kernel may reach another device: no remote copies, remote signals or barrier semaphores. Data moves between devices by JAX's collectives and lax.ppermute only.
A program may use at most 192 MiB of HBM per device.

```python
import math
import jax
import jax.numpy as jnp
import numpy as np
from jax import lax

NBAS = 16384
BLK = 128
SD = 2
BOXES = 4
BOX_PTS = 448
ATOMS = 3072
KNBR = 8
NB = 128
S_BOX = 16
RPO = 4
POINTS = 57344
N_PTS = 32
N_BAS = 8


def draw_screen(key, part):
    key = jax.random.fold_in(key, 11)
    key_list = jax.random.split(key, 3)
    box_rows = N_PTS * BOXES
    group = N_PTS // N_BAS
    slot_range = jnp.arange(S_BOX, dtype=jnp.int32) // SD
    slot_turn = jnp.arange(S_BOX, dtype=jnp.int32) % SD
    owner_pts = jnp.arange(box_rows, dtype=jnp.int32) // BOXES
    home_range = owner_pts // group
    own_scores = jax.random.randint(key_list[0], (box_rows, RPO), 0, 65536, dtype=jnp.int32) * RPO + jnp.arange(RPO, dtype=jnp.int32)[None, :]
    own_perm = jnp.argsort(own_scores, axis=1, stable=True).astype(jnp.int32)
    own_row = own_perm[:, slot_turn]
    far_scores = jax.random.randint(key_list[1], (N_PTS, N_BAS, group), 0, 65536, dtype=jnp.int32) * group + jnp.arange(group, dtype=jnp.int32)[None, None, :]
    far_perm = jnp.argsort(far_scores, axis=2, stable=True).astype(jnp.int32)
    far_owner = far_perm[owner_pts][:, slot_range, slot_turn]
    far_row = jax.random.randint(key_list[2], (box_rows, S_BOX), 0, RPO, dtype=jnp.int32)
    far_block = (slot_range[None, :] * group + far_owner) * RPO + far_row
    own_block = owner_pts[:, None] * RPO + own_row
    is_home = slot_range[None, :] == home_range[:, None]
    return jnp.where(is_home, own_block, far_block).astype(jnp.int32)


def set_ends(drawn, stream_key, smallest, top_value):
    index_at = [jax.random.randint(jax.random.fold_in(stream_key, axis), (), 0, length) for axis, length in enumerate(drawn.shape)]
    longest = drawn.shape.index(max(drawn.shape))
    beside = index_at[:longest] + [(index_at[longest] + 1) % drawn.shape[longest]] + index_at[longest + 1:]
    return drawn.at[tuple(index_at)].set(smallest).at[tuple(beside)].set(top_value)


def level_of(own_key, dims, shards, low, high):
    level, own = 1.0, jax.random.fold_in(own_key, 6)
    for position, shards_of in shards:
        heights = jnp.exp(jax.random.uniform(jax.random.fold_in(own, position), (shards_of,), jnp.float32, low / len(shards), high / len(shards)))
        level = level * jnp.repeat(heights, dims[position] // shards_of).reshape([-1 if axis == position else 1 for axis in range(len(dims))])
    return level


def profile(number_of, total, reach, skew):
    loads = [(1 << 20) // math.isqrt(rank ** skew) + 1 for rank in range(2, number_of + 1)]
    spare, holding = total - reach - (number_of - 1), [1] * (number_of - 1)
    while spare > 0:
        candidates = [i for i in range(number_of - 1) if holding[i] < reach]
        whole, left = sum([loads[i] for i in candidates]), spare
        for i in candidates:
            more = min(reach - holding[i], max(1, left * loads[i] // whole), spare)
            holding[i] = holding[i] + more
            spare = spare - more
    return np.array([reach] + holding)


def ragged(stream_key, count, total, reach, skew):
    if count == 2:
        one = jax.random.randint(stream_key, (), max(1, total - reach), min(reach, total - 1) + 1)
        return jnp.stack([one, total - one])
    tallies = jnp.asarray(profile(count, total, reach, skew), jnp.int32)
    pairs = (count - 1) // 2
    giver, sink = tallies[1:1 + 2 * pairs:2], tallies[2:2 + 2 * pairs:2]
    room = jnp.minimum(giver - 1, reach - sink)
    moved = jax.random.randint(jax.random.fold_in(stream_key, 1), (pairs,), 0, 1 << 20) % (room + 1)
    tallies = tallies.at[1:1 + 2 * pairs:2].set(giver - moved).at[2:2 + 2 * pairs:2].set(sink + moved)
    return tallies[jax.random.permutation(jax.random.fold_in(stream_key, 2), count)]


def normal_values(rng, dims, spread, bound, cuts=(), held_as=jnp.bfloat16):
    values = spread * jax.random.normal(rng, dims, jnp.float32)
    if cuts:
        values = values * level_of(rng, dims, cuts, -0.22, 0.18)
    return jnp.clip(values, -bound, bound).astype(held_as)


def setup_inputs(seed: int = 0) -> dict:
    streams_of = jax.random.split(jax.random.key(seed), 9)
    return {
        "chi": normal_values(streams_of[0], (N_PTS * BOXES, BOX_PTS, S_BOX * BLK), 1.0, 6.0, ((0, 32),)),
        "dchi": normal_values(streams_of[1], (3, N_PTS * BOXES, BOX_PTS, S_BOX * BLK), 1.0, 6.0, ((1, 32), (3, 8))),
        "screen": draw_screen(jax.random.fold_in(streams_of[8], 71), 0),
        "density": normal_values(streams_of[3], (NB, NB, BLK, BLK), (N_BAS * SD * BLK) ** -0.5, 0.125, ((0, 32), (1, 8))),
        "weights": jnp.clip(jnp.exp(math.log(0.02) - 2.30258502 * jax.random.uniform(streams_of[4], (N_PTS * BOXES, BOX_PTS), jnp.float32) ** level_of(streams_of[4], (N_PTS * BOXES, BOX_PTS), ((0, 32),), -0.2, 0.2)), 0.002, 0.02),
        "basis_atom": jnp.searchsorted(jnp.cumsum(ragged(streams_of[5], ATOMS, NBAS, 14, 1)), jnp.arange(NBAS), side="right").astype(jnp.int32),
        "neighbors": set_ends(jax.random.randint(streams_of[6], (KNBR, POINTS), 0, ATOMS), jax.random.fold_in(streams_of[6], 1), 0, ATOMS - 1).astype(jnp.int32),
        "weight_grad": normal_values(streams_of[7], (3, KNBR, POINTS), 0.003, 0.046875, ((2, 256),), jnp.float32),
    }


def reference(chi, dchi, screen, density, weights, basis_atom, neighbors, weight_grad):
    def one_box(box_item):
        chi_box, dchi_box, list_box, weight_box = box_item
        blocks = density[list_box[:, None], list_box[None, :]]
        values = chi_box.astype(jnp.float32).reshape(BOX_PTS, S_BOX, BLK)
        fock_rows = jnp.einsum("gsa,sjac->gjc", values, blocks.astype(jnp.float32)).reshape(BOX_PTS, S_BOX * BLK)
        energy = jnp.sum(chi_box.astype(jnp.float32) * fock_rows, axis=1)
        basis_term = -2.0 * jnp.sum(weight_box[None, :, None] * dchi_box.astype(jnp.float32) * fock_rows[None], axis=1)
        functions = (list_box[:, None] * BLK + jnp.arange(BLK, dtype=jnp.int32)[None, :]).reshape(-1)
        atom_ids = basis_atom[functions]
        return energy, basis_term, atom_ids

    dchi_boxes = jnp.moveaxis(dchi, 1, 0)
    energy, basis_term, atom_ids = lax.map(one_box, (chi, dchi_boxes, screen, weights))
    gradient = jnp.zeros((3, ATOMS), jnp.float32)
    basis_terms = jnp.moveaxis(basis_term, 1, 0).reshape(3, -1)
    gradient = gradient.at[:, atom_ids.reshape(-1)].add(basis_terms)
    becke_terms = (energy.reshape(-1)[None, None, :] * weight_grad).reshape(3, -1)
    gradient = gradient.at[:, neighbors.reshape(-1)].add(becke_terms)
    return gradient
```

```python
import jax
import jax.numpy as jnp
from jax import lax
from jax.sharding import PartitionSpec as P

ATOMS = 3072
CAPACITY = 4


def ranks_of(owner, valid):
    same = jnp.logical_and(owner[..., :, None] == owner[..., None, :], valid[..., None, :])
    count = owner.shape[-1]
    earlier = jnp.arange(count)[None, :] < jnp.arange(count)[:, None]
    return jnp.sum(jnp.logical_and(same, earlier).astype(jnp.int32), axis=-1)


def shards(chi, dchi, screen, density, weights, basis_atom, neighbors, weight_grad):
    box_count, box_pts, _ = chi.shape
    row_span, range_span, block_size, _ = density.shape
    n_pts = lax.axis_size("pts")
    n_bas = lax.axis_size("bas")
    slot_count = screen.shape[1]
    own_slots = slot_count // n_bas
    bas_index = lax.axis_index("bas")
    pts_index = lax.axis_index("pts")
    group = n_pts // n_bas
    home = pts_index // group
    flat = jnp.broadcast_to(screen.reshape(1, 1, -1), (n_pts, 1, box_count * slot_count))
    lists = lax.all_to_all(flat, "pts", split_axis=0, concat_axis=0, tiled=True)
    lists = lists.reshape(n_pts, box_count, slot_count)
    asked = lax.dynamic_slice_in_dim(lists, home * own_slots, own_slots, 2).reshape(n_pts, -1)
    columns = lax.dynamic_slice_in_dim(lists, bas_index * own_slots, own_slots, 2) - bas_index * range_span
    mine = asked // row_span == pts_index
    rank = ranks_of(asked // row_span, mine)
    place = jnp.arange(CAPACITY, dtype=jnp.int32)
    picked = jnp.logical_and(mine[:, None, :], rank[:, None, :] == place[None, :, None]).astype(jnp.int32)
    send_row = jnp.sum(picked * (asked % row_span)[:, None, :], axis=-1)
    entry_columns = jnp.repeat(columns, own_slots, axis=1)
    send_columns = jnp.sum(picked[..., None] * entry_columns[:, None], axis=2)
    outgoing = density[send_row[..., None], send_columns]
    arrived = lax.all_to_all(outgoing, "pts", split_axis=0, concat_axis=0, tiled=True)
    own_lists = screen.reshape(box_count, n_bas, own_slots).transpose(1, 0, 2).reshape(n_bas, -1)
    own_owner = own_lists // row_span
    own_place = jnp.minimum(ranks_of(own_owner, own_owner >= 0), CAPACITY - 1)
    index = own_owner * CAPACITY + own_place
    index = index.reshape(n_bas, box_count, own_slots).transpose(1, 0, 2).reshape(-1)
    fetched = arrived.reshape(n_pts * CAPACITY, own_slots, block_size, block_size)[index]
    fetched = fetched.reshape(box_count, slot_count, own_slots, block_size, block_size)
    own_columns = lax.dynamic_slice_in_dim(screen, bas_index * own_slots, own_slots, 1) - bas_index * range_span
    home_rows = lax.dynamic_slice_in_dim(screen, home * own_slots, own_slots, 1) - pts_index * row_span
    local = density[home_rows[:, :, None], own_columns[:, None, :]]
    chosen = lax.dynamic_update_slice_in_dim(fetched, local, home * own_slots, 1)
    values = chi.reshape(box_count, box_pts, slot_count, block_size)
    fock_rows = jnp.einsum("xgsa,xsjac->xgjc", values, chosen, preferred_element_type=jnp.float32)
    fock_rows = fock_rows.reshape(box_count, box_pts, own_slots * block_size)
    own_values = lax.dynamic_slice_in_dim(
        chi, bas_index * own_slots * block_size, own_slots * block_size, 2
    )
    energy_part = jnp.sum(own_values.astype(jnp.float32) * fock_rows, axis=2).reshape(n_bas, 1, -1)
    energy = jnp.sum(lax.all_to_all(energy_part, "bas", split_axis=0, concat_axis=0, tiled=True), axis=(0, 1))
    basis_term = -2.0 * jnp.sum(
        weights[None, :, :, None] * dchi.astype(jnp.float32) * fock_rows[None], axis=2
    )
    functions = (
        own_columns[:, :, None] * block_size + jnp.arange(block_size, dtype=jnp.int32)[None, None, :]
    ).reshape(box_count, -1)
    atom_ids = basis_atom[functions]
    gradient = jnp.zeros((3, ATOMS), jnp.float32)
    gradient = gradient.at[:, atom_ids.reshape(-1)].add(basis_term.reshape(3, -1))
    becke_terms = (energy[None, None, :] * weight_grad).reshape(3, -1)
    gradient = gradient.at[:, neighbors.reshape(-1)].add(becke_terms)
    devices = n_pts * n_bas
    parts = gradient.reshape(3, devices, -1).transpose(1, 0, 2).reshape(devices, 1, -1)
    parts = lax.all_to_all(parts, ("pts", "bas"), split_axis=0, concat_axis=0, tiled=True)
    return jnp.sum(parts, axis=(0, 1)).reshape(3, -1)


def solution(mesh):
    in_specs = (
        P("pts", None, None),
        P(None, "pts", None, "bas"),
        P("pts", None),
        P("pts", "bas", None, None),
        P("pts", None),
        P("bas"),
        P(None, ("pts", "bas")),
        P(None, None, ("pts", "bas")),
    )
    out_specs = P(None, ("pts", "bas"))
    return jax.shard_map(shards, mesh=mesh, in_specs=in_specs, out_specs=out_specs, check_vma=False)
```

```python
import functools

import jax
import jax.numpy as jnp
from jax import lax
from jax.experimental import pallas as pl
from jax.experimental.pallas import tpu as pltpu
from jax.sharding import PartitionSpec as P

CAPACITY = 4
MIB = 1024 * 1024


def send_kernel(lists_ref, density_ref, out_ref, sem, *, boxes, slots, own, rows, span):
    me = lax.axis_index("pts")
    bas = lax.axis_index("bas")
    home = lax.div(me, lax.axis_size("pts") // lax.axis_size("bas"))
    block = density_ref.shape[-1]

    def one_index(q, total):
        count = jnp.int32(0)
        for x in range(boxes):
            columns = [lists_ref[q, 0, x * slots + bas * own + j] - bas * span for j in range(own)]
            for t in range(own):
                wanted = lists_ref[q, 0, x * slots + home * own + t]
                row = wanted - me * rows
                mine = jnp.logical_and(row >= 0, row < rows)
                mine = jnp.logical_and(mine, jnp.logical_and(q != me, count < CAPACITY))

                @pl.when(mine)
                def _(row=row, columns=columns, count=count):
                    for j in range(own):
                        pltpu.make_async_copy(
                            density_ref.at[row, columns[j]],
                            out_ref.at[q, count, :, pl.ds(j * block, block)],
                            sem,
                        ).start()

                count = count + mine.astype(jnp.int32)
        return total + count

    total = lax.fori_loop(0, lists_ref.shape[0], one_index, jnp.int32(0))

    def drain(_, carry):
        for j in range(own):
            pltpu.make_async_copy(
                density_ref.at[0, 0], out_ref.at[0, 0, :, pl.ds(j * block, block)], sem
            ).wait()
        return carry

    lax.fori_loop(0, total, drain, 0)


def spread_kernel(atom_row_ref, column_ref, place_ref, value_ref, *, per_device, knbr):
    devices = place_ref.shape[1]
    owner = lax.broadcasted_iota(jnp.int32, (devices, 1), 0).astype(jnp.float32)
    place_ref[0] = jnp.where(owner == atom_row_ref[0], 1.0, 0.0).astype(jnp.bfloat16)
    lane = lax.broadcasted_iota(jnp.int32, (1, 128), 1)
    term = lax.rem(lane, 3 * per_device)
    axis = lax.div(term, per_device)
    inside = jnp.where(lane < 6 * per_device, (term - axis * per_device), -1).astype(jnp.float32)
    points = column_ref.shape[1]
    for k in range(knbr):
        cols = [column_ref[0, :, 4 * k + c : 4 * k + c + 1] for c in range(4)]
        value = jnp.where(axis == 0, cols[0], jnp.where(axis == 1, cols[1], cols[2]))
        value_ref[0, k * points : (k + 1) * points, :] = jnp.where(inside == cols[3], value, 0.0)


def split_parts(value, first):
    upper = value.astype(jnp.bfloat16).astype(jnp.float32)
    return jnp.where(first, upper, value - upper).astype(jnp.bfloat16)


def main_kernel(
    screen_ref,
    chi_ref,
    dchi_ref,
    arrived_ref,
    density_ref,
    weight_ref,
    atom_ref,
    place_ref,
    value_ref,
    out_ref,
    chi_buf,
    dchi_buf,
    block_buf,
    place_buf,
    value_buf,
    taken,
    chi_sem,
    dchi_sem,
    block_sem,
    place_sem,
    value_sem,
    *,
    rows,
    span,
    per_device,
):
    boxes, slots = screen_ref.shape
    block = density_ref.shape[-1]
    own = dchi_ref.shape[-1] // block
    me = lax.axis_index("pts")
    bas = lax.axis_index("bas")
    n_pts = lax.axis_size("pts")
    home = lax.div(me, n_pts // lax.axis_size("bas"))

    def chi_copy(x):
        return pltpu.make_async_copy(chi_ref.at[x], chi_buf.at[x], chi_sem.at[x])

    def dchi_copy(x):
        return pltpu.make_async_copy(dchi_ref.at[:, x], dchi_buf.at[x], dchi_sem.at[x])

    def place_copy(x):
        return pltpu.make_async_copy(place_ref.at[x], place_buf.at[x], place_sem.at[x])

    def value_copy(x):
        return pltpu.make_async_copy(value_ref.at[x], value_buf.at[x], value_sem.at[x])

    def clear(i, carry):
        taken[i] = 0
        return carry

    lax.fori_loop(0, n_pts, clear, 0)

    def block_copies(x):
        def one_slot(s, carry):
            wanted = screen_ref[x, s]
            owner = lax.div(wanted, rows)
            target = pl.ds(pl.multiple_of(s * block, block), block)

            @pl.when(owner == me)
            def _():
                for j in range(own):
                    column = screen_ref[x, bas * own + j] - bas * span
                    pltpu.make_async_copy(
                        density_ref.at[wanted - owner * rows, column],
                        block_buf.at[x, target, pl.ds(j * block, block)],
                        block_sem.at[x],
                    ).start()

            @pl.when(owner != me)
            def _():
                at = jnp.minimum(taken[owner], CAPACITY - 1)
                taken[owner] = at + 1
                pltpu.make_async_copy(
                    arrived_ref.at[owner, at], block_buf.at[x, target, :], block_sem.at[x]
                ).start()

            return carry

        lax.fori_loop(0, slots, one_slot, 0)

    for x in range(boxes):
        chi_copy(x).start()
        block_copies(x)
        dchi_copy(x).start()
        place_copy(x).start()
        value_copy(x).start()

    devices = out_ref.shape[0]
    owner_iota = lax.broadcasted_iota(jnp.int32, (devices, 1), 0)
    line = lax.broadcasted_iota(jnp.int32, (128, 1), 0)
    line_term = lax.rem(line, 3 * per_device)
    line_axis = lax.div(line_term, per_device)
    line_inside = jnp.where(line < 6 * per_device, line_term - line_axis * per_device, -1)
    lane = lax.broadcasted_iota(jnp.int32, (1, 128), 1)
    first_lane = lane < 3 * per_device
    first_line = line < 3 * per_device
    points = chi_buf.shape[1]
    knbr = value_buf.shape[1] // points
    total = jnp.zeros((devices, 128), jnp.float32)
    for x in range(boxes):
        chi_copy(x).wait()
        pltpu.make_async_copy(block_buf.at[x], block_buf.at[x], block_sem.at[x]).wait()
        fock = jnp.dot(chi_buf[x], block_buf[x], preferred_element_type=jnp.float32)
        width = own * block
        own_chi = chi_buf[x, :, pl.ds(pl.multiple_of(bas * width, width), width)]
        energy = jnp.sum(own_chi.astype(jnp.float32) * fock, axis=1, keepdims=True)
        weighted = fock * (-2.0 * weight_ref[x])
        dchi_copy(x).wait()
        terms = [
            jnp.sum(dchi_buf[x, d].astype(jnp.float32) * weighted, axis=0, keepdims=True)
            for d in range(3)
        ]
        atoms = jnp.concatenate(
            [
                atom_ref[pl.ds(screen_ref[x, bas * own + j] - bas * span, 1), :]
                for j in range(own)
            ],
            axis=1,
        )
        owners = lax.div(atoms, per_device)
        inside = atoms - owners * per_device
        spread = jnp.where(line_axis == 0, terms[0], jnp.where(line_axis == 1, terms[1], terms[2]))
        spread = jnp.where(line_inside == inside, spread, 0.0)
        onehot = jnp.where(owner_iota == owners, 1.0, 0.0).astype(jnp.bfloat16)
        total += lax.dot_general(
            onehot,
            split_parts(spread, first_line),
            (((1,), (1,)), ((), ())),
            preferred_element_type=jnp.float32,
        )
        place_copy(x).wait()
        value_copy(x).wait()
        becke = [
            split_parts(value_buf[x, k * points : (k + 1) * points, :] * energy, first_lane)
            for k in range(knbr)
        ]
        total += jnp.dot(
            place_buf[x], jnp.concatenate(becke, axis=0), preferred_element_type=jnp.float32
        )
    out_ref[...] = total + pltpu.roll(total, 128 - 3 * per_device, 1)


def shards(chi, dchi, screen, density, weights, basis_atom, neighbors, weight_grad):
    boxes, points, _ = chi.shape
    rows, span, block, _ = density.shape
    n_pts = lax.axis_size("pts")
    n_bas = lax.axis_size("bas")
    devices = n_pts * n_bas
    slots = screen.shape[1]
    own = slots // n_bas
    knbr = neighbors.shape[0]
    per_device = 12
    any_space = pl.BlockSpec(memory_space=pl.ANY)
    smem = pl.BlockSpec(memory_space=pltpu.SMEM)
    vmem = pl.BlockSpec(memory_space=pltpu.VMEM)

    flat = jnp.broadcast_to(screen.reshape(1, 1, -1), (n_pts, 1, boxes * slots))
    lists = lax.all_to_all(flat, "pts", split_axis=0, concat_axis=0, tiled=True)
    outgoing = pl.pallas_call(
        functools.partial(send_kernel, boxes=boxes, slots=slots, own=own, rows=rows, span=span),
        out_shape=jax.ShapeDtypeStruct((n_pts, CAPACITY, block, own * block), density.dtype),
        in_specs=[smem, any_space],
        out_specs=any_space,
        scratch_shapes=[pltpu.SemaphoreType.DMA],
        compiler_params=pltpu.CompilerParams(vmem_limit_bytes=4 * MIB),
    )(lists, density)
    arrived = lax.all_to_all(outgoing, "pts", split_axis=0, concat_axis=0, tiled=True)

    owner = neighbors // per_device
    packed = jnp.concatenate(
        [
            weight_grad,
            (neighbors - owner * per_device).astype(jnp.float32)[None],
            owner.astype(jnp.float32)[None],
        ]
    )
    packed = lax.all_gather(packed, "bas", axis=0)
    packed = packed.reshape(boxes, n_bas // boxes, 5, knbr, -1)
    columns = packed[:, :, :4].transpose(0, 1, 4, 3, 2).reshape(boxes, points, 4 * knbr)
    atom_rows = packed[:, :, 4].transpose(0, 2, 1, 3).reshape(boxes, 1, knbr * points)
    place, value = pl.pallas_call(
        functools.partial(spread_kernel, per_device=per_device, knbr=knbr),
        grid=(boxes,),
        out_shape=(
            jax.ShapeDtypeStruct((boxes, devices, knbr * points), jnp.bfloat16),
            jax.ShapeDtypeStruct((boxes, knbr * points, 128), jnp.float32),
        ),
        in_specs=[
            pl.BlockSpec((1, 1, knbr * points), lambda x: (x, 0, 0)),
            pl.BlockSpec((1, points, 4 * knbr), lambda x: (x, 0, 0)),
        ],
        out_specs=(
            pl.BlockSpec((1, devices, knbr * points), lambda x: (x, 0, 0)),
            pl.BlockSpec((1, knbr * points, 128), lambda x: (x, 0, 0)),
        ),
        compiler_params=pltpu.CompilerParams(vmem_limit_bytes=24 * MIB),
        cost_estimate=pl.CostEstimate(flops=20_000_000, bytes_accessed=16_000_000, transcendentals=0),
    )(atom_rows, columns)

    parts = pl.pallas_call(
        functools.partial(main_kernel, rows=rows, span=span, per_device=per_device),
        out_shape=jax.ShapeDtypeStruct((devices, 128), jnp.float32),
        in_specs=[smem] + [any_space] * 4 + [vmem] * 2 + [any_space] * 2,
        out_specs=vmem,
        scratch_shapes=[
            pltpu.VMEM(chi.shape, chi.dtype),
            pltpu.VMEM((boxes, 3) + dchi.shape[2:], dchi.dtype),
            pltpu.VMEM((boxes, slots * block, own * block), density.dtype),
            pltpu.VMEM(place.shape, place.dtype),
            pltpu.VMEM(value.shape, value.dtype),
            pltpu.SMEM((n_pts,), jnp.int32),
            pltpu.SemaphoreType.DMA((boxes,)),
            pltpu.SemaphoreType.DMA((boxes,)),
            pltpu.SemaphoreType.DMA((boxes,)),
            pltpu.SemaphoreType.DMA((boxes,)),
            pltpu.SemaphoreType.DMA((boxes,)),
        ],
        compiler_params=pltpu.CompilerParams(vmem_limit_bytes=52 * MIB),
        cost_estimate=pl.CostEstimate(flops=2_000_000_000, bytes_accessed=30_000_000, transcendentals=0),
    )(screen, chi, dchi, arrived, density, weights[:, :, None], basis_atom.reshape(span, block), place, value)
    parts = parts[:, : 3 * per_device].reshape(devices, 1, 3 * per_device)
    parts = lax.all_to_all(parts, ("pts", "bas"), split_axis=0, concat_axis=0, tiled=True)
    return jnp.sum(parts, axis=(0, 1)).reshape(3, -1)


def solution(mesh):
    in_specs = (
        P("pts", None, None),
        P(None, "pts", None, "bas"),
        P("pts", None),
        P("pts", "bas", None, None),
        P("pts", None),
        P("bas"),
        P(None, ("pts", "bas")),
        P(None, None, ("pts", "bas")),
    )
    out_specs = P(None, ("pts", "bas"))
    return jax.shard_map(shards, mesh=mesh, in_specs=in_specs, out_specs=out_specs, check_vma=False)
```

```python
import functools

import jax
import jax.numpy as jnp
from jax import lax
from jax.experimental import pallas as pl
from jax.experimental.pallas import tpu as pltpu
from jax.sharding import PartitionSpec as P

CAPACITY = 4
PACKED_ROWS = 2048
MIB = 1024 * 1024


def request_kernel(screen_hbm, table_ref, plan_ref, screen_ref, taken, sem, *, rows, span):
    load = pltpu.make_async_copy(screen_hbm, screen_ref, sem)
    load.start()
    boxes, slots = screen_ref.shape
    n_pts = table_ref.shape[0]
    me = lax.axis_index("pts")
    bas = lax.axis_index("bas")
    n_bas = lax.axis_size("bas")
    own = slots // n_bas
    home = lax.div(me, n_pts // n_bas)
    for i in range(n_pts):
        taken[i] = 0
        for c in range(CAPACITY):
            table_ref[i, 0, c] = 0
    load.wait()
    for x in range(boxes):
        columns = jnp.int32(0)
        for j in range(own):
            column = screen_ref[x, bas * own + j] - bas * span
            plan_ref[boxes * slots + x * 2 * own + j] = column
            plan_ref[boxes * slots + x * 2 * own + own + j] = screen_ref[x, home * own + j] - me * rows
            columns = columns * span + column
        for s in range(slots):
            wanted = screen_ref[x, s]
            owner = lax.shift_right_logical(wanted, rows.bit_length() - 1)
            at = taken[owner]
            taken[owner] = at + 1
            at = jnp.minimum(at, CAPACITY - 1)
            code = (wanted - owner * rows) * span**own + columns + 1
            table_ref[owner, 0, at] = jnp.where(owner == me, 0, code)
            plan_ref[x * slots + s] = owner * CAPACITY + at


def send_kernel(table_ref, density_ref, out_ref, sem, *, own):
    rows, span, block, _ = density_ref.shape

    def one_index(q, total):
        for c in range(CAPACITY):
            code = table_ref[q, 0, c]
            wanted = code > 0

            @pl.when(wanted)
            def _(code=code, c=c):
                rest = code - 1
                bits = span.bit_length() - 1
                row = jnp.bitwise_and(lax.shift_right_logical(rest, own * bits), rows - 1)
                for j in range(own):
                    shift = (own - 1 - j) * bits
                    column = jnp.bitwise_and(lax.shift_right_logical(rest, shift), span - 1)
                    pltpu.make_async_copy(
                        density_ref.at[row, column],
                        out_ref.at[q, c, :, pl.ds(j * block, block)],
                        sem,
                    ).start()

            total = total + wanted.astype(jnp.int32)
        return total

    total = lax.fori_loop(0, table_ref.shape[0], one_index, jnp.int32(0))

    def drain(_, carry):
        for j in range(own):
            pltpu.make_async_copy(
                density_ref.at[0, 0], out_ref.at[0, 0, :, pl.ds(j * block, block)], sem
            ).wait()
        return carry

    lax.fori_loop(0, total, drain, 0)


def pack_kernel(
    grad_ref,
    neighbor_ref,
    weight_ref,
    density_ref,
    packed_ref,
    weight_out_ref,
    density_out_ref,
    grad,
    neighbor,
    weight,
    turn,
    wide,
    tall,
    packed,
    sems,
    *,
    per_device,
):
    copies = [
        pltpu.make_async_copy(source, target, sems.at[i])
        for i, (source, target) in enumerate(
            [
                (grad_ref, grad),
                (neighbor_ref, neighbor),
                (weight_ref, weight),
                (density_ref, density_out_ref),
            ]
        )
    ]
    for copy in copies:
        copy.start()
    turn[...] = jnp.full_like(turn, -1.0)
    wide[...] = jnp.full_like(wide, -1.0)
    tall[...] = jnp.zeros_like(tall)
    for copy in copies[:3]:
        copy.wait()
    knbr, points = neighbor.shape
    owner = lax.div(neighbor[...], per_device)
    place = neighbor[...] - owner * per_device
    for d in range(3):
        wide[d, :, :points] = grad[d]
    wide[3, :, :points] = place.astype(jnp.float32)
    for c in range(4):
        for h in range(2):
            at = (c * 2 + h) * knbr
            packed[at : at + knbr, :] = wide[c, :, h * 128 : (h + 1) * 128]
    turn[:knbr, :points] = owner.astype(jnp.float32)
    packed[8 * knbr : 8 * knbr + 256, :] = turn[...].T
    packed_copy = pltpu.make_async_copy(packed, packed_ref.at[pl.ds(0, packed.shape[0])], sems.at[len(copies)])
    packed_copy.start()
    boxes, box_points = weight.shape
    tall[:boxes, :box_points] = weight[...]
    weight_out_ref[...] = tall[...].T[:box_points, :]
    for copy in copies[3:]:
        copy.wait()
    packed_copy.wait()


def in_hbm(array):
    return pltpu.with_memory_space_constraint(array, pltpu.HBM)


def spread_rows(values, places):
    inside = lax.broadcasted_iota(jnp.int32, (16, 1), 0).astype(jnp.float32) == places
    uppers, rests = [], []
    for value in values:
        upper = value.astype(jnp.bfloat16).astype(jnp.float32)
        uppers.append(jnp.where(inside, upper, 0.0))
        rests.append(jnp.where(inside, value - upper, 0.0))
    return jnp.concatenate(uppers + rests, axis=0).astype(jnp.bfloat16)


def owner_rows(owners, devices):
    line = lax.broadcasted_iota(jnp.int32, (devices, 1), 0).astype(jnp.float32).astype(jnp.bfloat16)
    one = jnp.ones((), jnp.bfloat16)
    zero = jnp.zeros((), jnp.bfloat16)
    return jnp.where(line == owners.astype(jnp.bfloat16), one, zero)


def along_lanes(left, right):
    return lax.dot_general(left, right, (((1,), (1,)), ((), ())), preferred_element_type=jnp.float32)


def main_kernel(
    plan_ref,
    chi_ref,
    dchi_ref,
    arrived_ref,
    density_ref,
    weight_ref,
    atom_ref,
    packed_ref,
    out_ref,
    chi_buf,
    block_buf,
    packed_buf,
    turn,
    chi_sem,
    block_sem,
    packed_sem,
    *,
    per_device,
    knbr,
):
    boxes = chi_buf.shape[0]
    block = density_ref.shape[-1]
    own = dchi_ref.shape[-1] // block
    slots = block_buf.shape[1] // block
    me = lax.axis_index("pts")
    bas = lax.axis_index("bas")
    n_bas = lax.axis_size("bas")
    halves = n_bas // boxes
    box_points = chi_buf.shape[1]
    points = box_points // halves
    devices = out_ref.shape[0]

    packed_copy = pltpu.make_async_copy(
        packed_ref.at[:, pl.ds(0, packed_buf.shape[1])], packed_buf, packed_sem
    )

    home = lax.div(me, lax.axis_size("pts") // n_bas)
    columns = [[plan_ref[boxes * slots + x * 2 * own + j] for j in range(own)] for x in range(boxes)]

    def block_copies(x):
        for i in range(slots):
            slot = lax.rem(home * own + i, slots)
            target = pl.ds(pl.multiple_of(slot * block, block), block)
            if i < own:
                row = plan_ref[boxes * slots + x * 2 * own + own + i]
                for j in range(own):
                    pltpu.make_async_copy(
                        density_ref.at[row, columns[x][j]],
                        block_buf.at[x, target, pl.ds(j * block, block)],
                        block_sem.at[x],
                    ).start()
            else:
                pltpu.make_async_copy(
                    arrived_ref.at[plan_ref[x * slots + slot]],
                    block_buf.at[x, target, :],
                    block_sem.at[x],
                ).start()

    def chi_copy(x):
        return pltpu.make_async_copy(chi_ref.at[x], chi_buf.at[x], chi_sem.at[x])

    for x in range(2):
        chi_copy(x).start()
        block_copies(x)
    packed_copy.start()

    owner_lane = lax.broadcasted_iota(jnp.int32, (1, devices), 1).astype(jnp.float32).astype(jnp.bfloat16)
    one = jnp.ones((), jnp.bfloat16)
    zero = jnp.zeros((), jnp.bfloat16)
    total = jnp.zeros((96, devices), jnp.float32)
    width = own * block
    for x in range(boxes):
        chi_copy(x).wait()
        pltpu.make_async_copy(block_buf.at[x], block_buf.at[x], block_sem.at[x]).wait()
        fock = jnp.dot(chi_buf[x], block_buf[x], preferred_element_type=jnp.float32)
        if x + 2 < boxes:
            chi_copy(x + 2).start()
            block_copies(x + 2)
        own_chi = chi_buf[x, :, pl.ds(pl.multiple_of(bas * width, width), width)]
        energy = jnp.sum(own_chi.astype(jnp.float32) * fock, axis=1, keepdims=True)
        weighted = fock * (-2.0 * weight_ref[:, x : x + 1])
        terms = [
            jnp.sum(dchi_ref[d, x].astype(jnp.float32) * weighted, axis=0, keepdims=True)
            for d in range(3)
        ]
        atoms = jnp.concatenate(
            [
                atom_ref[pl.ds(columns[x][j], 1), :]
                for j in range(own)
            ],
            axis=1,
        )
        owners = lax.div(atoms, per_device)
        inside = (atoms - owners * per_device).astype(jnp.float32)
        total += along_lanes(
            spread_rows(terms, inside), owner_rows(owners.astype(jnp.float32), devices)
        )
        if x == 0:
            packed_copy.wait()
        for h in range(halves):
            at = x * halves + h
            turn[:points, :] = jnp.broadcast_to(energy[h * points : (h + 1) * points], (points, 128))
            energy_row = turn[...].T[0:1, :]
            energy_row = jnp.where(
                lax.broadcasted_iota(jnp.int32, energy_row.shape, 1) < points, energy_row, 0.0
            )

            def lanes(c, at=at):
                return jnp.concatenate(
                    [packed_buf[at, (c * 2 + p) * knbr : (c * 2 + p + 1) * knbr, :] for p in range(2)],
                    axis=1,
                )

            grads = [lanes(d) * energy_row for d in range(3)]
            places = lanes(3)
            owners = packed_buf[at, 8 * knbr : 8 * knbr + 256, :].astype(jnp.bfloat16)
            left = jnp.concatenate(
                [
                    spread_rows([g[k : k + 1] for g in grads], places[k : k + 1])
                    for k in range(knbr)
                ],
                axis=1,
            )
            right = jnp.concatenate(
                [
                    jnp.where(owner_lane == owners[:, k : k + 1], one, zero)
                    for k in range(knbr)
                ],
                axis=0,
            )
            total += jnp.dot(left, right, preferred_element_type=jnp.float32)
    both = total[:48] + total[48:]
    parts = [both[d * 16 : d * 16 + per_device] for d in range(3)]
    parts.append(jnp.zeros((128 - 3 * per_device, devices), jnp.float32))
    out_ref[...] = jnp.concatenate(parts, axis=0).T


def run_main(plan, chi, dchi, arrived, density, weight_lines, atoms, gathered, devices, per_device):
    boxes = chi.shape[0]
    block = density.shape[-1]
    own = dchi.shape[-1] // block
    slots = chi.shape[-1] // block
    n_bas = lax.axis_size("bas")
    knbr = 8
    hbm = pl.BlockSpec(memory_space=pltpu.HBM)
    smem = pl.BlockSpec(memory_space=pltpu.SMEM)
    vmem = pl.BlockSpec(memory_space=pltpu.VMEM)
    return pl.pallas_call(
        functools.partial(main_kernel, per_device=per_device, knbr=knbr),
        out_shape=jax.ShapeDtypeStruct((devices, 128), jnp.float32),
        in_specs=[smem] + [hbm, vmem] + [hbm] * 2 + [vmem] * 2 + [hbm],
        out_specs=vmem,
        scratch_shapes=[
            pltpu.VMEM(chi.shape, chi.dtype),
            pltpu.VMEM((boxes, slots * block, own * block), density.dtype),
            pltpu.VMEM((n_bas, 8 * knbr + 256, 128), jnp.float32),
            pltpu.VMEM((256, 128), jnp.float32),
            pltpu.SemaphoreType.DMA((boxes,)),
            pltpu.SemaphoreType.DMA((boxes,)),
            pltpu.SemaphoreType.DMA,
        ],
        compiler_params=pltpu.CompilerParams(vmem_limit_bytes=28 * MIB),
        cost_estimate=pl.CostEstimate(flops=2_000_000_000, bytes_accessed=30_000_000, transcendentals=0),
    )(
        plan,
        chi,
        dchi,
        arrived,
        density,
        weight_lines,
        atoms,
        gathered,
    )


def shards(chi, dchi, screen, density, weights, basis_atom, neighbors, weight_grad):
    boxes, points, _ = chi.shape
    rows, span, block, _ = density.shape
    n_pts = lax.axis_size("pts")
    n_bas = lax.axis_size("bas")
    devices = n_pts * n_bas
    slots = screen.shape[1]
    own = slots // n_bas
    knbr = neighbors.shape[0]
    per_device = 12
    hbm = pl.BlockSpec(memory_space=pltpu.HBM)
    smem = pl.BlockSpec(memory_space=pltpu.SMEM)
    vmem = pl.BlockSpec(memory_space=pltpu.VMEM)

    table, plan = pl.pallas_call(
        functools.partial(request_kernel, rows=rows, span=span),
        out_shape=(
            jax.ShapeDtypeStruct((n_pts, 1, CAPACITY), jnp.int32),
            jax.ShapeDtypeStruct((boxes * (slots + 2 * own),), jnp.int32),
        ),
        in_specs=[hbm],
        out_specs=(smem, smem),
        scratch_shapes=[
            pltpu.SMEM(screen.shape, jnp.int32),
            pltpu.SMEM((n_pts,), jnp.int32),
            pltpu.SemaphoreType.DMA,
        ],
        compiler_params=pltpu.CompilerParams(vmem_limit_bytes=4 * MIB),
    )(in_hbm(screen))
    asked = lax.all_to_all(table, "pts", split_axis=0, concat_axis=0, tiled=True)
    packed, weight_lines, loaded = pl.pallas_call(
        functools.partial(pack_kernel, per_device=per_device),
        out_shape=(
            pltpu.HBM((PACKED_ROWS, 128), jnp.float32),
            jax.ShapeDtypeStruct((points, 128), jnp.float32),
            pltpu.VMEM(density.shape, density.dtype),
        ),
        in_specs=[hbm] * 4,
        out_specs=(hbm, vmem, vmem),
        scratch_shapes=[
            pltpu.VMEM(weight_grad.shape, jnp.float32),
            pltpu.VMEM(neighbors.shape, jnp.int32),
            pltpu.VMEM(weights.shape, jnp.float32),
            pltpu.VMEM((128, 256), jnp.float32),
            pltpu.VMEM((4, knbr, 256), jnp.float32),
            pltpu.VMEM((128, 512), jnp.float32),
            pltpu.VMEM((8 * knbr + 256, 128), jnp.float32),
            pltpu.SemaphoreType.DMA((5,)),
        ],
        compiler_params=pltpu.CompilerParams(vmem_limit_bytes=16 * MIB),
        cost_estimate=pl.CostEstimate(flops=5_000_000, bytes_accessed=2_000_000, transcendentals=0),
    )(
        in_hbm(weight_grad),
        in_hbm(neighbors),
        in_hbm(weights),
        in_hbm(density),
    )
    asked, weight_lines, packed = lax.optimization_barrier((asked, weight_lines, packed))
    gathered = in_hbm(lax.all_gather(packed, "bas", axis=0))
    outgoing = pl.pallas_call(
        functools.partial(send_kernel, own=own),
        out_shape=pltpu.HBM((n_pts, CAPACITY, block, own * block), density.dtype),
        in_specs=[smem, vmem],
        out_specs=hbm,
        scratch_shapes=[pltpu.SemaphoreType.DMA],
        compiler_params=pltpu.CompilerParams(vmem_limit_bytes=4 * MIB),
    )(asked, loaded)
    arrived = lax.all_to_all(outgoing, "pts", split_axis=0, concat_axis=0, tiled=True)

    parts = run_main(
        plan,
        in_hbm(chi),
        dchi,
        in_hbm(arrived.reshape(n_pts * CAPACITY, block, own * block)),
        in_hbm(density),
        weight_lines,
        basis_atom.reshape(span, block),
        gathered,
        devices,
        per_device,
    )
    parts = parts[:, : 3 * per_device].reshape(devices, 1, 3 * per_device)
    parts = lax.all_to_all(parts, ("pts", "bas"), split_axis=0, concat_axis=0, tiled=True)
    return jnp.sum(parts, axis=(0, 1)).reshape(3, per_device)


def solution(mesh):
    in_specs = (
        P("pts", None, None),
        P(None, "pts", None, "bas"),
        P("pts", None),
        P("pts", "bas", None, None),
        P("pts", None),
        P("bas"),
        P(None, ("pts", "bas")),
        P(None, None, ("pts", "bas")),
    )
    out_specs = P(None, ("pts", "bas"))
    return jax.shard_map(shards, mesh=mesh, in_specs=in_specs, out_specs=out_specs, check_vma=False)
```

```python
import functools

import jax
import jax.numpy as jnp
from jax import lax
from jax.experimental import pallas as pl
from jax.experimental.pallas import tpu as pltpu
from jax.sharding import PartitionSpec as P

PACKED_ROWS = 1024
MIB = 1024 * 1024


def first_kernel(
    density_ref,
    screen_ref,
    grad_ref,
    neighbor_ref,
    weight_ref,
    *refs,
    group,
    per_device,
):
    outs = refs[:group]
    packed_ref, weight_out_ref, lists_ref = refs[group : group + 3]
    held, grad, neighbor, weight, screen, turn, wide, tall, packed, load_sem, sem, small_sem = refs[group + 3 :]
    part = density_ref.shape[2] // group
    place = lax.rem(lax.axis_index("pts"), group)
    rows = density_ref.shape[0]
    loads = [
        pltpu.make_async_copy(density_ref.at[i], held.at[i], load_sem.at[i]) for i in range(rows)
    ]
    small = [
        pltpu.make_async_copy(source, target, small_sem.at[i])
        for i, (source, target) in enumerate(
            [(screen_ref, screen), (grad_ref, grad), (neighbor_ref, neighbor), (weight_ref, weight)]
        )
    ]
    for load in loads:
        load.start()
    for load in small:
        load.start()
    turn[...] = jnp.full_like(turn, -1.0)
    wide[...] = jnp.full_like(wide, -1.0)
    tall[...] = jnp.zeros_like(tall)
    copies = []
    for i in range(rows):
        loads[i].wait()
        for d in reversed(range(group)):
            start = pl.multiple_of(jnp.bitwise_xor(place, d) * part, part)
            copies.append(
                pltpu.make_async_copy(held.at[i, :, pl.ds(start, part)], outs[d].at[i], sem.at[d, i])
            )
            copies[-1].start()
    for load in small:
        load.wait()
    boxes, slots = screen.shape
    line = jnp.concatenate([screen[x : x + 1, :] for x in range(boxes)], axis=1)
    for q in range(lists_ref.shape[0]):
        lists_ref[q] = line
    knbr, points = neighbor.shape
    owner = lax.div(neighbor[...], per_device)
    inside = neighbor[...] - owner * per_device
    for d in range(3):
        wide[d, :, :points] = grad[d]
    wide[3, :, :points] = inside.astype(jnp.float32)
    for c in range(4):
        for h in range(2):
            at = (c * 2 + h) * knbr
            packed[at : at + knbr, :] = wide[c, :, h * 128 : (h + 1) * 128]
    turn[:knbr, :points] = owner.astype(jnp.float32)
    packed[8 * knbr : 8 * knbr + 256, :] = turn[...].T
    packed_copy = pltpu.make_async_copy(packed, packed_ref.at[pl.ds(0, packed.shape[0])], small_sem.at[4])
    packed_copy.start()
    boxes, box_points = weight.shape
    tall[:boxes, :box_points] = weight[...]
    weight_out_ref[...] = tall[...].T[:box_points, :]
    for copy in copies:
        copy.wait()
    packed_copy.wait()


def send_kernel(lists_ref, *refs, boxes, slots, own):
    *pieces, out_ref, held, stage, load_sem, sem = refs
    group = len(pieces)
    rows, span = pieces[0].shape[:2]
    block = held.shape[-1]
    me = lax.axis_index("pts")
    bas = lax.axis_index("bas")
    place = lax.rem(me, group)
    home = lax.div(me, group)
    loads = []
    for d, piece in enumerate(pieces):
        start = jnp.bitwise_xor(place, d) * rows
        loads.append(pltpu.make_async_copy(piece, held.at[pl.ds(start, rows)], load_sem.at[d]))
        loads[-1].start()
    for load in loads:
        load.wait()

    def one_index(q, carry):
        found = []
        for x in range(boxes):
            columns = [lists_ref[q, 0, x * slots + bas * own + j] - bas * span for j in range(own)]
            for t in range(own):
                row = lists_ref[q, 0, x * slots + home * own + t] - home * group * rows
                found.append([held[row, columns[j]] for j in range(own)])
        for i, parts in enumerate(found):
            stage[q, i] = jnp.concatenate(parts, axis=1)
        pltpu.make_async_copy(stage.at[q], out_ref.at[q], sem).start()
        return carry

    lax.fori_loop(0, lists_ref.shape[0], one_index, 0, unroll=2)
    pltpu.make_async_copy(stage, out_ref, sem).wait()


def in_hbm(array):
    return pltpu.with_memory_space_constraint(array, pltpu.HBM)


def spread_rows(values, places):
    inside = lax.broadcasted_iota(jnp.int32, (16, 1), 0).astype(jnp.float32) == places
    uppers, rests = [], []
    for value in values:
        upper = value.astype(jnp.bfloat16).astype(jnp.float32)
        uppers.append(jnp.where(inside, upper, 0.0))
        rests.append(jnp.where(inside, value - upper, 0.0))
    return jnp.concatenate(uppers + rests, axis=0).astype(jnp.bfloat16)


def owner_rows(owners, devices):
    line = lax.broadcasted_iota(jnp.int32, (devices, 1), 0).astype(jnp.float32).astype(jnp.bfloat16)
    one = jnp.ones((), jnp.bfloat16)
    zero = jnp.zeros((), jnp.bfloat16)
    return jnp.where(line == owners.astype(jnp.bfloat16), one, zero)


def along_lanes(left, right):
    return lax.dot_general(left, right, (((1,), (1,)), ((), ())), preferred_element_type=jnp.float32)


def main_kernel(
    screen_ref,
    chi_ref,
    dchi_ref,
    arrived_ref,
    weight_ref,
    atom_ref,
    packed_ref,
    out_ref,
    chi_buf,
    block_buf,
    packed_buf,
    turn,
    chi_sem,
    block_sem,
    packed_sem,
    *,
    per_device,
    knbr,
):
    boxes = chi_buf.shape[0]
    span, block = atom_ref.shape
    own = dchi_ref.shape[-1] // block
    bas = lax.axis_index("bas")
    n_bas = lax.axis_size("bas")
    halves = n_bas // boxes
    box_points = chi_buf.shape[1]
    points = box_points // halves
    devices = out_ref.shape[0]

    packed_copy = pltpu.make_async_copy(
        packed_ref.at[:, pl.ds(0, packed_buf.shape[1])], packed_buf, packed_sem
    )
    columns = [[screen_ref[x, bas * own + j] - bas * span for j in range(own)] for x in range(boxes)]

    def block_copies(x):
        for t in range(own):
            pltpu.make_async_copy(
                arrived_ref.at[:, :, x * own + t], block_buf.at[x, :, t], block_sem.at[x]
            ).start()

    def chi_copy(x):
        return pltpu.make_async_copy(chi_ref.at[x], chi_buf.at[x], chi_sem.at[x])

    for x in range(2):
        chi_copy(x).start()
        block_copies(x)
    packed_copy.start()

    owner_lane = lax.broadcasted_iota(jnp.int32, (1, devices), 1).astype(jnp.float32).astype(jnp.bfloat16)
    one = jnp.ones((), jnp.bfloat16)
    zero = jnp.zeros((), jnp.bfloat16)
    total = jnp.zeros((96, devices), jnp.float32)
    width = own * block
    for x in range(boxes):
        chi_copy(x).wait()
        pltpu.make_async_copy(block_buf.at[x], block_buf.at[x], block_sem.at[x]).wait()
        blocks = block_buf[x].reshape(chi_buf.shape[2], own * block)
        fock = jnp.dot(chi_buf[x], blocks, preferred_element_type=jnp.float32)
        if x + 2 < boxes:
            chi_copy(x + 2).start()
            block_copies(x + 2)
        own_chi = chi_buf[x, :, pl.ds(pl.multiple_of(bas * width, width), width)]
        energy = jnp.sum(own_chi.astype(jnp.float32) * fock, axis=1, keepdims=True)
        weighted = fock * (-2.0 * weight_ref[:, x : x + 1])
        terms = [
            jnp.sum(dchi_ref[d, x].astype(jnp.float32) * weighted, axis=0, keepdims=True)
            for d in range(3)
        ]
        atoms = jnp.concatenate(
            [
                atom_ref[pl.ds(columns[x][j], 1), :]
                for j in range(own)
            ],
            axis=1,
        )
        owners = lax.div(atoms, per_device)
        inside = (atoms - owners * per_device).astype(jnp.float32)
        total += along_lanes(
            spread_rows(terms, inside), owner_rows(owners.astype(jnp.float32), devices)
        )
        if x == 0:
            packed_copy.wait()
        for h in range(halves):
            at = x * halves + h
            turn[:points, :] = jnp.broadcast_to(energy[h * points : (h + 1) * points], (points, 128))
            energy_row = turn[...].T[0:1, :]
            energy_row = jnp.where(
                lax.broadcasted_iota(jnp.int32, energy_row.shape, 1) < points, energy_row, 0.0
            )

            def lanes(c, at=at):
                return jnp.concatenate(
                    [packed_buf[at, (c * 2 + p) * knbr : (c * 2 + p + 1) * knbr, :] for p in range(2)],
                    axis=1,
                )

            grads = [lanes(d) * energy_row for d in range(3)]
            places = lanes(3)
            owners = packed_buf[at, 8 * knbr : 8 * knbr + 256, :].astype(jnp.bfloat16)
            left = jnp.concatenate(
                [
                    spread_rows([g[k : k + 1] for g in grads], places[k : k + 1])
                    for k in range(knbr)
                ],
                axis=1,
            )
            right = jnp.concatenate(
                [
                    jnp.where(owner_lane == owners[:, k : k + 1], one, zero)
                    for k in range(knbr)
                ],
                axis=0,
            )
            total += jnp.dot(left, right, preferred_element_type=jnp.float32)
    both = total[:48] + total[48:]
    parts = [both[d * 16 : d * 16 + per_device] for d in range(3)]
    parts.append(jnp.zeros((128 - 3 * per_device, devices), jnp.float32))
    out_ref[...] = jnp.concatenate(parts, axis=0).T


def run_main(screen, chi, dchi, arrived, weight_lines, atoms, gathered, devices, per_device):
    boxes = chi.shape[0]
    n_bas = lax.axis_size("bas")
    knbr = 8
    hbm = pl.BlockSpec(memory_space=pltpu.HBM)
    smem = pl.BlockSpec(memory_space=pltpu.SMEM)
    vmem = pl.BlockSpec(memory_space=pltpu.VMEM)
    ranges, group, asked, part, width = arrived.shape
    return pl.pallas_call(
        functools.partial(main_kernel, per_device=per_device, knbr=knbr),
        out_shape=jax.ShapeDtypeStruct((devices, 128), jnp.float32),
        in_specs=[smem, hbm, vmem, hbm, vmem, vmem, hbm],
        out_specs=vmem,
        scratch_shapes=[
            pltpu.VMEM(chi.shape, chi.dtype),
            pltpu.VMEM((boxes, ranges, asked // boxes, group, part, width), arrived.dtype),
            pltpu.VMEM((n_bas, 8 * knbr + 256, 128), jnp.float32),
            pltpu.VMEM((256, 128), jnp.float32),
            pltpu.SemaphoreType.DMA((boxes,)),
            pltpu.SemaphoreType.DMA((boxes,)),
            pltpu.SemaphoreType.DMA,
        ],
        compiler_params=pltpu.CompilerParams(vmem_limit_bytes=28 * MIB),
        cost_estimate=pl.CostEstimate(flops=2_000_000_000, bytes_accessed=30_000_000, transcendentals=0),
    )(
        screen,
        chi,
        dchi,
        arrived,
        weight_lines,
        atoms,
        gathered,
    )


def shards(chi, dchi, screen, density, weights, basis_atom, neighbors, weight_grad):
    boxes, points, _ = chi.shape
    rows, span, block, _ = density.shape
    n_pts = lax.axis_size("pts")
    n_bas = lax.axis_size("bas")
    devices = n_pts * n_bas
    slots = screen.shape[1]
    own = slots // n_bas
    knbr = neighbors.shape[0]
    per_device = 12
    hbm = pl.BlockSpec(memory_space=pltpu.HBM)
    smem = pl.BlockSpec(memory_space=pltpu.SMEM)
    vmem = pl.BlockSpec(memory_space=pltpu.VMEM)

    group = n_pts // n_bas
    *pieces, packed, weight_lines, flat = pl.pallas_call(
        functools.partial(first_kernel, group=group, per_device=per_device),
        out_shape=[pltpu.HBM((rows, span, block // group, block), density.dtype)] * group
        + [
            pltpu.HBM((PACKED_ROWS, 128), jnp.float32),
            jax.ShapeDtypeStruct((points, 128), jnp.float32),
            jax.ShapeDtypeStruct((n_pts, 1, boxes * slots), jnp.int32),
        ],
        in_specs=[hbm] * 5,
        out_specs=[hbm] * (group + 1) + [vmem] * 2,
        scratch_shapes=[
            pltpu.VMEM(density.shape, density.dtype),
            pltpu.VMEM(weight_grad.shape, jnp.float32),
            pltpu.VMEM(neighbors.shape, jnp.int32),
            pltpu.VMEM(weights.shape, jnp.float32),
            pltpu.VMEM(screen.shape, jnp.int32),
            pltpu.VMEM((128, 256), jnp.float32),
            pltpu.VMEM((4, knbr, 256), jnp.float32),
            pltpu.VMEM((128, 512), jnp.float32),
            pltpu.VMEM((8 * knbr + 256, 128), jnp.float32),
            pltpu.SemaphoreType.DMA((rows,)),
            pltpu.SemaphoreType.DMA((group, rows)),
            pltpu.SemaphoreType.DMA((5,)),
        ],
        compiler_params=pltpu.CompilerParams(vmem_limit_bytes=12 * MIB),
    )(in_hbm(density), in_hbm(screen), in_hbm(weight_grad), in_hbm(neighbors), in_hbm(weights))
    pieces = [in_hbm(pieces[0])] + [
        lax.ppermute(pieces[d], "pts", [(p, p ^ d) for p in range(n_pts)]) for d in range(1, group)
    ]
    lists = lax.all_to_all(flat, "pts", split_axis=0, concat_axis=0, tiled=True)
    gathered = in_hbm(lax.all_gather(packed, "bas", axis=0))
    outgoing = pl.pallas_call(
        functools.partial(send_kernel, boxes=boxes, slots=slots, own=own),
        out_shape=pltpu.HBM((n_pts, boxes * own, block // group, own * block), density.dtype),
        in_specs=[smem] + [hbm] * group,
        out_specs=hbm,
        scratch_shapes=[
            pltpu.VMEM((group * rows, span, block // group, block), density.dtype),
            pltpu.VMEM((n_pts, boxes * own, block // group, own * block), density.dtype),
            pltpu.SemaphoreType.DMA((group,)),
            pltpu.SemaphoreType.DMA,
        ],
        compiler_params=pltpu.CompilerParams(vmem_limit_bytes=12 * MIB),
    )(lists, *pieces)
    arrived = lax.all_to_all(outgoing, "pts", split_axis=0, concat_axis=0, tiled=True)
    arrived = arrived.reshape(n_bas, group, boxes * own, block // group, own * block)

    parts = run_main(
        screen,
        in_hbm(chi),
        dchi,
        in_hbm(arrived),
        weight_lines,
        basis_atom.reshape(span, block),
        gathered,
        devices,
        per_device,
    )
    parts = parts[:, : 3 * per_device].reshape(devices, 1, 3 * per_device)
    parts = lax.all_to_all(parts, ("pts", "bas"), split_axis=0, concat_axis=0, tiled=True)
    return jnp.sum(parts, axis=(0, 1)).reshape(3, per_device)


def solution(mesh):
    in_specs = (
        P("pts", None, None),
        P(None, "pts", None, "bas"),
        P("pts", None),
        P("pts", "bas", None, None),
        P("pts", None),
        P("bas"),
        P(None, ("pts", "bas")),
        P(None, None, ("pts", "bas")),
    )
    out_specs = P(None, ("pts", "bas"))
    return jax.shard_map(shards, mesh=mesh, in_specs=in_specs, out_specs=out_specs, check_vma=False)
```

```python
import functools

import jax
import jax.numpy as jnp
from jax import lax
from jax.experimental import pallas as pl
from jax.experimental.pallas import tpu as pltpu
from jax.sharding import PartitionSpec as P

MIB = 1024 * 1024


def first_kernel(
    density_ref,
    screen_ref,
    grad_ref,
    neighbor_ref,
    *refs,
    group,
):
    outs = refs[:group]
    packed_ref, lists_ref = refs[group : group + 2]
    held, grad, neighbor, screen, wide, load_sem, sem, small_sem = refs[group + 2 :]
    part = density_ref.shape[2] // group
    place = lax.rem(lax.axis_index("pts"), group)
    rows = density_ref.shape[0]
    loads = [
        pltpu.make_async_copy(density_ref.at[i], held.at[i], load_sem.at[i]) for i in range(rows)
    ]
    small = [
        pltpu.make_async_copy(source, target, small_sem.at[i])
        for i, (source, target) in enumerate(
            [(screen_ref, screen), (grad_ref, grad), (neighbor_ref, neighbor)]
        )
    ]
    for load in loads:
        load.start()
    for load in small:
        load.start()
    wide[...] = jnp.full_like(wide, -1.0)
    copies = []
    for i in range(rows):
        loads[i].wait()
        for d in reversed(range(group)):
            start = pl.multiple_of(jnp.bitwise_xor(place, d) * part, part)
            copies.append(
                pltpu.make_async_copy(held.at[i, :, pl.ds(start, part)], outs[d].at[i], sem.at[d, i])
            )
            copies[-1].start()
    for load in small:
        load.wait()
    boxes, slots = screen.shape
    line = jnp.concatenate([screen[x : x + 1, :] for x in range(boxes)], axis=1)
    for q in range(lists_ref.shape[0]):
        lists_ref[q] = line
    knbr, points = neighbor.shape
    for d in range(3):
        wide[d, :, :points] = grad[d]
    wide[3, :, :points] = neighbor[...].astype(jnp.float32)
    for c in range(4):
        for h in range(2):
            at = (c * 2 + h) * knbr
            packed_ref[at : at + knbr, :] = wide[c, :, h * 128 : (h + 1) * 128]
    for copy in copies:
        copy.wait()


def unpack_kernel(packed_ref, weight_ref, out_ref, weight_out_ref, turn, tall, *, per_device, knbr):
    turn[...] = jnp.zeros_like(turn)
    for at in range(packed_ref.shape[0]):
        out_ref[at, : 6 * knbr, :] = packed_ref[at, : 6 * knbr, :]
        for h in range(2):
            rows = slice((6 + h) * knbr, (7 + h) * knbr)
            atoms = packed_ref[at, rows, :].astype(jnp.int32)
            owner = lax.div(atoms, per_device)
            out_ref[at, rows, :] = (atoms - owner * per_device).astype(jnp.float32)
            turn[at, :knbr, h * 128 : (h + 1) * 128] = owner.astype(jnp.float32)
        out_ref[at, 8 * knbr :, :] = turn[at].T
    tall[...] = jnp.zeros_like(tall)
    boxes, box_points = weight_ref.shape
    tall[:boxes, :box_points] = weight_ref[...]
    weight_out_ref[...] = tall[...].T[:box_points, :]


def send_kernel(lists_ref, *refs, boxes, slots, own):
    *pieces, out_ref, held, stage, load_sem, sem = refs
    group = len(pieces)
    rows, span = pieces[0].shape[:2]
    block = held.shape[-1]
    me = lax.axis_index("pts")
    bas = lax.axis_index("bas")
    place = lax.rem(me, group)
    home = lax.div(me, group)
    loads = []
    for d, piece in enumerate(pieces):
        start = jnp.bitwise_xor(place, d) * rows
        loads.append(pltpu.make_async_copy(piece, held.at[pl.ds(start, rows)], load_sem.at[d]))
        loads[-1].start()
    for load in loads:
        load.wait()

    def one_index(q, carry):
        found = []
        for x in range(boxes):
            columns = [lists_ref[q, 0, x * slots + bas * own + j] - bas * span for j in range(own)]
            for t in range(own):
                row = lists_ref[q, 0, x * slots + home * own + t] - home * group * rows
                found.append([held[row, columns[j]] for j in range(own)])
        for i, parts in enumerate(found):
            stage[q, i] = jnp.concatenate(parts, axis=1)
        pltpu.make_async_copy(stage.at[q], out_ref.at[q], sem).start()
        return carry

    lax.fori_loop(0, lists_ref.shape[0], one_index, 0, unroll=2)
    pltpu.make_async_copy(stage, out_ref, sem).wait()


def in_hbm(array):
    return pltpu.with_memory_space_constraint(array, pltpu.HBM)


def spread_rows(values, places):
    inside = lax.broadcasted_iota(jnp.int32, (16, 1), 0).astype(jnp.float32) == places
    uppers, rests = [], []
    for value in values:
        upper = value.astype(jnp.bfloat16).astype(jnp.float32)
        uppers.append(jnp.where(inside, upper, 0.0))
        rests.append(jnp.where(inside, value - upper, 0.0))
    return jnp.concatenate(uppers + rests, axis=0).astype(jnp.bfloat16)


def owner_rows(owners, devices):
    line = lax.broadcasted_iota(jnp.int32, (devices, 1), 0).astype(jnp.float32).astype(jnp.bfloat16)
    one = jnp.ones((), jnp.bfloat16)
    zero = jnp.zeros((), jnp.bfloat16)
    return jnp.where(line == owners.astype(jnp.bfloat16), one, zero)


def along_lanes(left, right):
    return lax.dot_general(left, right, (((1,), (1,)), ((), ())), preferred_element_type=jnp.float32)


def main_kernel(
    screen_ref,
    chi_ref,
    dchi_ref,
    arrived_ref,
    weight_ref,
    atom_ref,
    packed_ref,
    out_ref,
    chi_buf,
    block_buf,
    packed_buf,
    turn,
    chi_sem,
    block_sem,
    packed_sem,
    *,
    per_device,
    knbr,
):
    boxes = chi_buf.shape[0]
    span, block = atom_ref.shape
    own = dchi_ref.shape[-1] // block
    bas = lax.axis_index("bas")
    n_bas = lax.axis_size("bas")
    halves = n_bas // boxes
    box_points = chi_buf.shape[1]
    points = box_points // halves
    devices = out_ref.shape[0]

    packed_copy = pltpu.make_async_copy(
        packed_ref, packed_buf, packed_sem
    )
    columns = [[screen_ref[x, bas * own + j] - bas * span for j in range(own)] for x in range(boxes)]

    def block_copies(x):
        for t in range(own):
            pltpu.make_async_copy(
                arrived_ref.at[:, :, x * own + t], block_buf.at[x, :, t], block_sem.at[x]
            ).start()

    def chi_copy(x):
        return pltpu.make_async_copy(chi_ref.at[x], chi_buf.at[x], chi_sem.at[x])

    for x in range(2):
        chi_copy(x).start()
        block_copies(x)
    packed_copy.start()

    owner_lane = lax.broadcasted_iota(jnp.int32, (1, devices), 1).astype(jnp.float32).astype(jnp.bfloat16)
    one = jnp.ones((), jnp.bfloat16)
    zero = jnp.zeros((), jnp.bfloat16)
    total = jnp.zeros((96, devices), jnp.float32)
    width = own * block
    for x in range(boxes):
        chi_copy(x).wait()
        pltpu.make_async_copy(block_buf.at[x], block_buf.at[x], block_sem.at[x]).wait()
        blocks = block_buf[x].reshape(chi_buf.shape[2], own * block)
        fock = jnp.dot(chi_buf[x], blocks, preferred_element_type=jnp.float32)
        if x + 2 < boxes:
            chi_copy(x + 2).start()
            block_copies(x + 2)
        own_chi = chi_buf[x, :, pl.ds(pl.multiple_of(bas * width, width), width)]
        energy = jnp.sum(own_chi.astype(jnp.float32) * fock, axis=1, keepdims=True)
        weighted = fock * (-2.0 * weight_ref[:, x : x + 1])
        terms = [
            jnp.sum(dchi_ref[d, x].astype(jnp.float32) * weighted, axis=0, keepdims=True)
            for d in range(3)
        ]
        atoms = jnp.concatenate(
            [
                atom_ref[pl.ds(columns[x][j], 1), :]
                for j in range(own)
            ],
            axis=1,
        )
        owners = lax.div(atoms, per_device)
        inside = (atoms - owners * per_device).astype(jnp.float32)
        total += along_lanes(
            spread_rows(terms, inside), owner_rows(owners.astype(jnp.float32), devices)
        )
        if x == 0:
            packed_copy.wait()
        for h in range(halves):
            at = x * halves + h
            turn[:points, :] = jnp.broadcast_to(energy[h * points : (h + 1) * points], (points, 128))
            energy_row = turn[...].T[0:1, :]
            energy_row = jnp.where(
                lax.broadcasted_iota(jnp.int32, energy_row.shape, 1) < points, energy_row, 0.0
            )

            def lanes(c, at=at):
                return jnp.concatenate(
                    [packed_buf[at, (c * 2 + p) * knbr : (c * 2 + p + 1) * knbr, :] for p in range(2)],
                    axis=1,
                )

            grads = [lanes(d) * energy_row for d in range(3)]
            places = lanes(3)
            owners = packed_buf[at, 8 * knbr : 8 * knbr + 256, :].astype(jnp.bfloat16)
            left = jnp.concatenate(
                [
                    spread_rows([g[k : k + 1] for g in grads], places[k : k + 1])
                    for k in range(knbr)
                ],
                axis=1,
            )
            right = jnp.concatenate(
                [
                    jnp.where(owner_lane == owners[:, k : k + 1], one, zero)
                    for k in range(knbr)
                ],
                axis=0,
            )
            total += jnp.dot(left, right, preferred_element_type=jnp.float32)
    both = total[:48] + total[48:]
    parts = [both[d * 16 : d * 16 + per_device] for d in range(3)]
    parts.append(jnp.zeros((128 - 3 * per_device, devices), jnp.float32))
    out_ref[...] = jnp.concatenate(parts, axis=0).T


def run_main(screen, chi, dchi, arrived, weight_lines, atoms, gathered, devices, per_device):
    boxes = chi.shape[0]
    n_bas = lax.axis_size("bas")
    knbr = 8
    hbm = pl.BlockSpec(memory_space=pltpu.HBM)
    smem = pl.BlockSpec(memory_space=pltpu.SMEM)
    vmem = pl.BlockSpec(memory_space=pltpu.VMEM)
    ranges, group, asked, part, width = arrived.shape
    return pl.pallas_call(
        functools.partial(main_kernel, per_device=per_device, knbr=knbr),
        out_shape=jax.ShapeDtypeStruct((devices, 128), jnp.float32),
        in_specs=[smem, hbm, vmem, hbm, vmem, vmem, hbm],
        out_specs=vmem,
        scratch_shapes=[
            pltpu.VMEM(chi.shape, chi.dtype),
            pltpu.VMEM((boxes, ranges, asked // boxes, group, part, width), arrived.dtype),
            pltpu.VMEM((n_bas, 8 * knbr + 256, 128), jnp.float32),
            pltpu.VMEM((256, 128), jnp.float32),
            pltpu.SemaphoreType.DMA((boxes,)),
            pltpu.SemaphoreType.DMA((boxes,)),
            pltpu.SemaphoreType.DMA,
        ],
        compiler_params=pltpu.CompilerParams(vmem_limit_bytes=28 * MIB),
        cost_estimate=pl.CostEstimate(flops=2_000_000_000, bytes_accessed=30_000_000, transcendentals=0),
    )(
        screen,
        chi,
        dchi,
        arrived,
        weight_lines,
        atoms,
        gathered,
    )


def shards(chi, dchi, screen, density, weights, basis_atom, neighbors, weight_grad):
    boxes, points, _ = chi.shape
    rows, span, block, _ = density.shape
    n_pts = lax.axis_size("pts")
    n_bas = lax.axis_size("bas")
    devices = n_pts * n_bas
    slots = screen.shape[1]
    own = slots // n_bas
    knbr = neighbors.shape[0]
    per_device = 12
    hbm = pl.BlockSpec(memory_space=pltpu.HBM)
    smem = pl.BlockSpec(memory_space=pltpu.SMEM)
    vmem = pl.BlockSpec(memory_space=pltpu.VMEM)

    group = n_pts // n_bas
    *pieces, packed, flat = pl.pallas_call(
        functools.partial(first_kernel, group=group),
        out_shape=[pltpu.HBM((rows, span, block // group, block), density.dtype)] * group
        + [
            jax.ShapeDtypeStruct((8 * knbr, 128), jnp.float32),
            jax.ShapeDtypeStruct((n_pts, 1, boxes * slots), jnp.int32),
        ],
        in_specs=[hbm] * 4,
        out_specs=[hbm] * group + [vmem] * 2,
        scratch_shapes=[
            pltpu.VMEM(density.shape, density.dtype),
            pltpu.VMEM(weight_grad.shape, jnp.float32),
            pltpu.VMEM(neighbors.shape, jnp.int32),
            pltpu.VMEM(screen.shape, jnp.int32),
            pltpu.VMEM((4, knbr, 256), jnp.float32),
            pltpu.SemaphoreType.DMA((rows,)),
            pltpu.SemaphoreType.DMA((group, rows)),
            pltpu.SemaphoreType.DMA((3,)),
        ],
        compiler_params=pltpu.CompilerParams(vmem_limit_bytes=12 * MIB),
    )(in_hbm(density), in_hbm(screen), in_hbm(weight_grad), in_hbm(neighbors))
    pieces = [in_hbm(pieces[0])] + [
        lax.ppermute(pieces[d], "pts", [(p, p ^ d) for p in range(n_pts)]) for d in range(1, group)
    ]
    lists = lax.all_to_all(flat, "pts", split_axis=0, concat_axis=0, tiled=True)
    unpacked, weight_lines = pl.pallas_call(
        functools.partial(unpack_kernel, per_device=per_device, knbr=knbr),
        out_shape=(
            jax.ShapeDtypeStruct((n_bas, 8 * knbr + 256, 128), jnp.float32),
            jax.ShapeDtypeStruct((points, 128), jnp.float32),
        ),
        in_specs=[vmem] * 2,
        out_specs=(vmem, vmem),
        scratch_shapes=[
            pltpu.VMEM((n_bas, 128, 256), jnp.float32),
            pltpu.VMEM((128, 512), jnp.float32),
        ],
        compiler_params=pltpu.CompilerParams(vmem_limit_bytes=12 * MIB),
        cost_estimate=pl.CostEstimate(flops=5_000_000, bytes_accessed=4_000_000, transcendentals=0),
    )(lax.all_gather(packed, "bas", axis=0), weights)
    outgoing = pl.pallas_call(
        functools.partial(send_kernel, boxes=boxes, slots=slots, own=own),
        out_shape=pltpu.HBM((n_pts, boxes * own, block // group, own * block), density.dtype),
        in_specs=[smem] + [hbm] * group,
        out_specs=hbm,
        scratch_shapes=[
            pltpu.VMEM((group * rows, span, block // group, block), density.dtype),
            pltpu.VMEM((n_pts, boxes * own, block // group, own * block), density.dtype),
            pltpu.SemaphoreType.DMA((group,)),
            pltpu.SemaphoreType.DMA,
        ],
        compiler_params=pltpu.CompilerParams(vmem_limit_bytes=12 * MIB),
    )(lists, *pieces)
    arrived = lax.all_to_all(outgoing, "pts", split_axis=0, concat_axis=0, tiled=True)
    arrived = arrived.reshape(n_bas, group, boxes * own, block // group, own * block)

    parts = run_main(
        screen,
        in_hbm(chi),
        dchi,
        in_hbm(arrived),
        weight_lines,
        basis_atom.reshape(span, block),
        in_hbm(unpacked),
        devices,
        per_device,
    )
    parts = parts[:, : 3 * per_device].reshape(devices, 1, 3 * per_device)
    parts = lax.all_to_all(parts, ("pts", "bas"), split_axis=0, concat_axis=0, tiled=True)
    return jnp.sum(parts, axis=(0, 1)).reshape(3, per_device)


def solution(mesh):
    in_specs = (
        P("pts", None, None),
        P(None, "pts", None, "bas"),
        P("pts", None),
        P("pts", "bas", None, None),
        P("pts", None),
        P("bas"),
        P(None, ("pts", "bas")),
        P(None, None, ("pts", "bas")),
    )
    out_specs = P(None, ("pts", "bas"))
    return jax.shard_map(shards, mesh=mesh, in_specs=in_specs, out_specs=out_specs, check_vma=False)
```

```python
import functools

import jax
import jax.numpy as jnp
from jax import lax
from jax.experimental import pallas as pl
from jax.experimental.pallas import tpu as pltpu
from jax.sharding import PartitionSpec as P

MIB = 1024 * 1024


def first_kernel(
    density_ref,
    screen_ref,
    grad_ref,
    neighbor_ref,
    *refs,
    group,
):
    outs = refs[:group]
    packed_ref, lists_ref = refs[group : group + 2]
    held, grad, neighbor, screen, wide, load_sem, sem, small_sem = refs[group + 2 :]
    part = density_ref.shape[2] // group
    place = lax.rem(lax.axis_index("pts"), group)
    rows = density_ref.shape[0]
    loads = [
        pltpu.make_async_copy(density_ref.at[i], held.at[i], load_sem.at[i]) for i in range(rows)
    ]
    small = [
        pltpu.make_async_copy(source, target, small_sem.at[i])
        for i, (source, target) in enumerate(
            [(screen_ref, screen), (grad_ref, grad), (neighbor_ref, neighbor)]
        )
    ]
    for load in loads:
        load.start()
    for load in small:
        load.start()
    wide[...] = jnp.full_like(wide, -1.0)
    copies = []
    for i in range(rows):
        loads[i].wait()
        for d in reversed(range(group)):
            start = pl.multiple_of(jnp.bitwise_xor(place, d) * part, part)
            copies.append(
                pltpu.make_async_copy(held.at[i, :, pl.ds(start, part)], outs[d].at[i], sem.at[d, i])
            )
            copies[-1].start()
    for load in small:
        load.wait()
    boxes, slots = screen.shape
    line = jnp.concatenate([screen[x : x + 1, :] for x in range(boxes)], axis=1)
    for q in range(lists_ref.shape[0]):
        lists_ref[q] = line
    knbr, points = neighbor.shape
    for d in range(3):
        wide[d, :, :points] = grad[d]
    wide[3, :, :points] = neighbor[...].astype(jnp.float32)
    for c in range(4):
        for h in range(2):
            at = (c * 2 + h) * knbr
            packed_ref[at : at + knbr, :] = wide[c, :, h * 128 : (h + 1) * 128]
    for copy in copies:
        copy.wait()


def unpack_kernel(packed_ref, weight_ref, out_ref, weight_out_ref, turn, tall, *, per_device, knbr):
    turn[...] = jnp.zeros_like(turn)
    for at in range(packed_ref.shape[0]):
        out_ref[at, : 6 * knbr, :] = packed_ref[at, : 6 * knbr, :]
        for h in range(2):
            rows = slice((6 + h) * knbr, (7 + h) * knbr)
            atoms = packed_ref[at, rows, :].astype(jnp.int32)
            owner = lax.div(atoms, per_device)
            out_ref[at, rows, :] = (atoms - owner * per_device).astype(jnp.float32)
            turn[at, :knbr, h * 128 : (h + 1) * 128] = owner.astype(jnp.float32)
        out_ref[at, 8 * knbr :, :] = turn[at].T
    tall[...] = jnp.zeros_like(tall)
    boxes, box_points = weight_ref.shape
    tall[:boxes, :box_points] = weight_ref[...]
    weight_out_ref[...] = tall[...].T[:box_points, :]


def send_kernel(lists_hbm, *refs, boxes, slots, own):
    *pieces, out_ref, lists_ref, held, stage, lists_sem, load_sem, sem = refs
    lists_load = pltpu.make_async_copy(lists_hbm, lists_ref, lists_sem)
    lists_load.start()
    group = len(pieces)
    rows, span = pieces[0].shape[:2]
    block = held.shape[-1]
    me = lax.axis_index("pts")
    bas = lax.axis_index("bas")
    place = lax.rem(me, group)
    home = lax.div(me, group)
    loads = []
    for d, piece in enumerate(pieces):
        start = jnp.bitwise_xor(place, d) * rows
        loads.append(pltpu.make_async_copy(piece, held.at[pl.ds(start, rows)], load_sem.at[d]))
        loads[-1].start()
    lists_load.wait()
    for load in loads:
        load.wait()

    def one_index(q, carry):
        found = []
        for x in range(boxes):
            columns = [lists_ref[q, 0, x * slots + bas * own + j] - bas * span for j in range(own)]
            for t in range(own):
                row = lists_ref[q, 0, x * slots + home * own + t] - home * group * rows
                found.append([held[row, columns[j]] for j in range(own)])
        for i, parts in enumerate(found):
            stage[q, i] = jnp.concatenate(parts, axis=1)
        pltpu.make_async_copy(stage.at[q], out_ref.at[q], sem).start()
        return carry

    lax.fori_loop(0, lists_ref.shape[0], one_index, 0, unroll=8)
    pltpu.make_async_copy(stage, out_ref, sem).wait()


def in_hbm(array):
    return pltpu.with_memory_space_constraint(array, pltpu.HBM)


def spread_rows(values, places):
    inside = lax.broadcasted_iota(jnp.int32, (16, 1), 0).astype(jnp.float32) == places
    uppers, rests = [], []
    for value in values:
        upper = value.astype(jnp.bfloat16).astype(jnp.float32)
        uppers.append(jnp.where(inside, upper, 0.0))
        rests.append(jnp.where(inside, value - upper, 0.0))
    return jnp.concatenate(uppers + rests, axis=0).astype(jnp.bfloat16)


def owner_rows(owners, devices):
    line = lax.broadcasted_iota(jnp.int32, (devices, 1), 0).astype(jnp.float32).astype(jnp.bfloat16)
    one = jnp.ones((), jnp.bfloat16)
    zero = jnp.zeros((), jnp.bfloat16)
    return jnp.where(line == owners.astype(jnp.bfloat16), one, zero)


def along_lanes(left, right):
    return lax.dot_general(left, right, (((1,), (1,)), ((), ())), preferred_element_type=jnp.float32)


def main_kernel(
    screen_hbm,
    chi_ref,
    dchi_ref,
    arrived_ref,
    weight_ref,
    atom_ref,
    packed_ref,
    out_ref,
    chi_buf,
    block_buf,
    packed_buf,
    turn,
    screen_ref,
    screen_sem,
    chi_sem,
    block_sem,
    packed_sem,
    *,
    per_device,
    knbr,
):
    boxes = chi_buf.shape[0]
    span, block = atom_ref.shape
    own = dchi_ref.shape[-1] // block
    bas = lax.axis_index("bas")
    n_bas = lax.axis_size("bas")
    halves = n_bas // boxes
    box_points = chi_buf.shape[1]
    points = box_points // halves
    devices = out_ref.shape[0]

    packed_copy = pltpu.make_async_copy(
        packed_ref, packed_buf, packed_sem
    )
    screen_copy = pltpu.make_async_copy(screen_hbm, screen_ref, screen_sem)
    screen_copy.start()

    def block_copies(x):
        for t in range(own):
            pltpu.make_async_copy(
                arrived_ref.at[:, :, x * own + t], block_buf.at[x, :, t], block_sem.at[x]
            ).start()

    def chi_copy(x):
        return pltpu.make_async_copy(chi_ref.at[x], chi_buf.at[x], chi_sem.at[x])

    for x in range(2):
        chi_copy(x).start()
        block_copies(x)
    packed_copy.start()
    screen_copy.wait()
    columns = [[screen_ref[x, bas * own + j] - bas * span for j in range(own)] for x in range(boxes)]

    owner_lane = lax.broadcasted_iota(jnp.int32, (1, devices), 1).astype(jnp.float32).astype(jnp.bfloat16)
    one = jnp.ones((), jnp.bfloat16)
    zero = jnp.zeros((), jnp.bfloat16)
    total = jnp.zeros((96, devices), jnp.float32)
    width = own * block
    for x in range(boxes):
        chi_copy(x).wait()
        pltpu.make_async_copy(block_buf.at[x], block_buf.at[x], block_sem.at[x]).wait()
        blocks = block_buf[x].reshape(chi_buf.shape[2], own * block)
        fock = jnp.dot(chi_buf[x], blocks, preferred_element_type=jnp.float32)
        if x + 2 < boxes:
            chi_copy(x + 2).start()
            block_copies(x + 2)
        own_chi = chi_buf[x, :, pl.ds(pl.multiple_of(bas * width, width), width)]
        energy = jnp.sum(own_chi.astype(jnp.float32) * fock, axis=1, keepdims=True)
        weighted = fock * (-2.0 * weight_ref[:, x : x + 1])
        terms = [
            jnp.sum(dchi_ref[d, x].astype(jnp.float32) * weighted, axis=0, keepdims=True)
            for d in range(3)
        ]
        atoms = jnp.concatenate(
            [
                atom_ref[pl.ds(columns[x][j], 1), :]
                for j in range(own)
            ],
            axis=1,
        )
        owners = lax.div(atoms, per_device)
        inside = (atoms - owners * per_device).astype(jnp.float32)
        total += along_lanes(
            spread_rows(terms, inside), owner_rows(owners.astype(jnp.float32), devices)
        )
        if x == 0:
            packed_copy.wait()
        for h in range(halves):
            at = x * halves + h
            turn[:points, :] = jnp.broadcast_to(energy[h * points : (h + 1) * points], (points, 128))
            energy_row = turn[...].T[0:1, :]
            energy_row = jnp.where(
                lax.broadcasted_iota(jnp.int32, energy_row.shape, 1) < points, energy_row, 0.0
            )

            def lanes(c, at=at):
                return jnp.concatenate(
                    [packed_buf[at, (c * 2 + p) * knbr : (c * 2 + p + 1) * knbr, :] for p in range(2)],
                    axis=1,
                )

            grads = [lanes(d) * energy_row for d in range(3)]
            places = lanes(3)
            owners = packed_buf[at, 8 * knbr : 8 * knbr + 256, :].astype(jnp.bfloat16)
            left = jnp.concatenate(
                [
                    spread_rows([g[k : k + 1] for g in grads], places[k : k + 1])
                    for k in range(knbr)
                ],
                axis=1,
            )
            right = jnp.concatenate(
                [
                    jnp.where(owner_lane == owners[:, k : k + 1], one, zero)
                    for k in range(knbr)
                ],
                axis=0,
            )
            total += jnp.dot(left, right, preferred_element_type=jnp.float32)
    both = total[:48] + total[48:]
    parts = [both[d * 16 : d * 16 + per_device] for d in range(3)]
    parts.append(jnp.zeros((128 - 3 * per_device, devices), jnp.float32))
    out_ref[...] = jnp.concatenate(parts, axis=0).T


def run_main(screen, chi, dchi, arrived, weight_lines, atoms, gathered, devices, per_device):
    boxes = chi.shape[0]
    n_bas = lax.axis_size("bas")
    knbr = 8
    hbm = pl.BlockSpec(memory_space=pltpu.HBM)
    vmem = pl.BlockSpec(memory_space=pltpu.VMEM)
    ranges, group, asked, part, width = arrived.shape
    return pl.pallas_call(
        functools.partial(main_kernel, per_device=per_device, knbr=knbr),
        out_shape=jax.ShapeDtypeStruct((devices, 128), jnp.float32),
        in_specs=[hbm, hbm, vmem, hbm, vmem, vmem, hbm],
        out_specs=vmem,
        scratch_shapes=[
            pltpu.VMEM(chi.shape, chi.dtype),
            pltpu.VMEM((boxes, ranges, asked // boxes, group, part, width), arrived.dtype),
            pltpu.VMEM((n_bas, 8 * knbr + 256, 128), jnp.float32),
            pltpu.VMEM((256, 128), jnp.float32),
            pltpu.SMEM(screen.shape, jnp.int32),
            pltpu.SemaphoreType.DMA,
            pltpu.SemaphoreType.DMA((boxes,)),
            pltpu.SemaphoreType.DMA((boxes,)),
            pltpu.SemaphoreType.DMA,
        ],
        compiler_params=pltpu.CompilerParams(vmem_limit_bytes=28 * MIB),
        cost_estimate=pl.CostEstimate(flops=2_000_000_000, bytes_accessed=30_000_000, transcendentals=0),
    )(
        screen,
        chi,
        dchi,
        arrived,
        weight_lines,
        atoms,
        gathered,
    )


def shards(chi, dchi, screen, density, weights, basis_atom, neighbors, weight_grad):
    boxes, points, _ = chi.shape
    rows, span, block, _ = density.shape
    n_pts = lax.axis_size("pts")
    n_bas = lax.axis_size("bas")
    devices = n_pts * n_bas
    slots = screen.shape[1]
    own = slots // n_bas
    knbr = neighbors.shape[0]
    per_device = 12
    hbm = pl.BlockSpec(memory_space=pltpu.HBM)
    vmem = pl.BlockSpec(memory_space=pltpu.VMEM)

    group = n_pts // n_bas
    *pieces, packed, flat = pl.pallas_call(
        functools.partial(first_kernel, group=group),
        out_shape=[pltpu.HBM((rows, span, block // group, block), density.dtype)] * group
        + [
            jax.ShapeDtypeStruct((8 * knbr, 128), jnp.float32),
            jax.ShapeDtypeStruct((n_pts, 1, boxes * slots), jnp.int32),
        ],
        in_specs=[hbm] * 4,
        out_specs=[hbm] * group + [vmem] * 2,
        scratch_shapes=[
            pltpu.VMEM(density.shape, density.dtype),
            pltpu.VMEM(weight_grad.shape, jnp.float32),
            pltpu.VMEM(neighbors.shape, jnp.int32),
            pltpu.VMEM(screen.shape, jnp.int32),
            pltpu.VMEM((4, knbr, 256), jnp.float32),
            pltpu.SemaphoreType.DMA((rows,)),
            pltpu.SemaphoreType.DMA((group, rows)),
            pltpu.SemaphoreType.DMA((3,)),
        ],
        compiler_params=pltpu.CompilerParams(vmem_limit_bytes=12 * MIB),
    )(in_hbm(density), in_hbm(screen), in_hbm(weight_grad), in_hbm(neighbors))
    pieces = [in_hbm(pieces[0])] + [
        lax.ppermute(pieces[d], "pts", [(p, p ^ d) for p in range(n_pts)]) for d in range(1, group)
    ]
    lists = lax.all_to_all(flat, "pts", split_axis=0, concat_axis=0, tiled=True)
    unpacked, weight_lines = pl.pallas_call(
        functools.partial(unpack_kernel, per_device=per_device, knbr=knbr),
        out_shape=(
            jax.ShapeDtypeStruct((n_bas, 8 * knbr + 256, 128), jnp.float32),
            jax.ShapeDtypeStruct((points, 128), jnp.float32),
        ),
        in_specs=[vmem] * 2,
        out_specs=(vmem, vmem),
        scratch_shapes=[
            pltpu.VMEM((n_bas, 128, 256), jnp.float32),
            pltpu.VMEM((128, 512), jnp.float32),
        ],
        compiler_params=pltpu.CompilerParams(vmem_limit_bytes=12 * MIB),
        cost_estimate=pl.CostEstimate(flops=5_000_000, bytes_accessed=4_000_000, transcendentals=0),
    )(lax.all_gather(packed, "bas", axis=0), weights)
    outgoing = pl.pallas_call(
        functools.partial(send_kernel, boxes=boxes, slots=slots, own=own),
        out_shape=pltpu.HBM((n_pts, boxes * own, block // group, own * block), density.dtype),
        in_specs=[hbm] * (group + 1),
        out_specs=hbm,
        scratch_shapes=[
            pltpu.SMEM(lists.shape, jnp.int32),
            pltpu.VMEM((group * rows, span, block // group, block), density.dtype),
            pltpu.VMEM((n_pts, boxes * own, block // group, own * block), density.dtype),
            pltpu.SemaphoreType.DMA,
            pltpu.SemaphoreType.DMA((group,)),
            pltpu.SemaphoreType.DMA,
        ],
        compiler_params=pltpu.CompilerParams(vmem_limit_bytes=12 * MIB),
    )(lists, *pieces)
    arrived = lax.all_to_all(outgoing, "pts", split_axis=0, concat_axis=0, tiled=True)
    arrived = arrived.reshape(n_bas, group, boxes * own, block // group, own * block)

    parts = run_main(
        in_hbm(screen),
        in_hbm(chi),
        dchi,
        in_hbm(arrived),
        weight_lines,
        basis_atom.reshape(span, block),
        in_hbm(unpacked),
        devices,
        per_device,
    )
    parts = parts[:, : 3 * per_device].reshape(devices, 1, 3 * per_device)
    parts = lax.all_to_all(parts, ("pts", "bas"), split_axis=0, concat_axis=0, tiled=True)
    return jnp.sum(parts, axis=(0, 1)).reshape(3, per_device)


def solution(mesh):
    in_specs = (
        P("pts", None, None),
        P(None, "pts", None, "bas"),
        P("pts", None),
        P("pts", "bas", None, None),
        P("pts", None),
        P("bas"),
        P(None, ("pts", "bas")),
        P(None, None, ("pts", "bas")),
    )
    out_specs = P(None, ("pts", "bas"))
    return jax.shard_map(shards, mesh=mesh, in_specs=in_specs, out_specs=out_specs, check_vma=False)
```

```python
import functools

import jax
import jax.numpy as jnp
from jax import lax
from jax.experimental import pallas as pl
from jax.experimental.pallas import tpu as pltpu
from jax.sharding import PartitionSpec as P

MIB = 1024 * 1024


def first_kernel(
    density_ref,
    screen_ref,
    grad_ref,
    neighbor_ref,
    *refs,
    group,
):
    outs = refs[:group]
    packed_ref, lists_ref = refs[group : group + 2]
    held, grad, neighbor, screen, wide, load_sem, sem, small_sem = refs[group + 2 :]
    part = density_ref.shape[2] // group
    place = lax.rem(lax.axis_index("pts"), group)
    rows = density_ref.shape[0]
    loads = [
        pltpu.make_async_copy(density_ref.at[i], held.at[i], load_sem.at[i]) for i in range(rows)
    ]
    small = [
        pltpu.make_async_copy(source, target, small_sem.at[i])
        for i, (source, target) in enumerate(
            [(screen_ref, screen), (grad_ref, grad), (neighbor_ref, neighbor)]
        )
    ]
    for load in loads:
        load.start()
    for load in small:
        load.start()
    wide[...] = jnp.full_like(wide, -1.0)
    copies = []
    for i in range(rows):
        loads[i].wait()
        for d in reversed(range(group)):
            start = pl.multiple_of(jnp.bitwise_xor(place, d) * part, part)
            copies.append(
                pltpu.make_async_copy(held.at[i, :, pl.ds(start, part)], outs[d].at[i], sem.at[d, i])
            )
            copies[-1].start()
    for load in small:
        load.wait()
    boxes, slots = screen.shape
    line = jnp.concatenate([screen[x : x + 1, :] for x in range(boxes)], axis=1)
    for q in range(lists_ref.shape[0]):
        lists_ref[q] = line
    knbr, points = neighbor.shape
    for d in range(3):
        wide[d, :, :points] = grad[d]
    wide[3, :, :points] = neighbor[...].astype(jnp.float32)
    for c in range(4):
        for h in range(2):
            at = (c * 2 + h) * knbr
            packed_ref[at : at + knbr, :] = wide[c, :, h * 128 : (h + 1) * 128]
    for copy in copies:
        copy.wait()


def unpack_kernel(packed_ref, weight_ref, out_ref, weight_out_ref, turn, tall, *, per_device, knbr):
    turn[...] = jnp.zeros_like(turn)
    for at in range(packed_ref.shape[0]):
        out_ref[at, : 6 * knbr, :] = packed_ref[at, : 6 * knbr, :]
        for h in range(2):
            rows = slice((6 + h) * knbr, (7 + h) * knbr)
            atoms = packed_ref[at, rows, :].astype(jnp.int32)
            owner = lax.div(atoms, per_device)
            out_ref[at, rows, :] = (atoms - owner * per_device).astype(jnp.float32)
            turn[at, :knbr, h * 128 : (h + 1) * 128] = owner.astype(jnp.float32)
        out_ref[at, 8 * knbr :, :] = turn[at].T
    tall[...] = jnp.zeros_like(tall)
    boxes, box_points = weight_ref.shape
    tall[:boxes, :box_points] = weight_ref[...]
    weight_out_ref[...] = tall[...].T[:box_points, :]


def send_kernel(lists_hbm, *refs, boxes, slots, own):
    *pieces, out_ref, lists_ref, held, stage, lists_sem, load_sem, sem = refs
    lists_load = pltpu.make_async_copy(lists_hbm, lists_ref, lists_sem)
    lists_load.start()
    group = len(pieces)
    rows, span = pieces[0].shape[:2]
    block = held.shape[-1]
    me = lax.axis_index("pts")
    bas = lax.axis_index("bas")
    place = lax.rem(me, group)
    home = lax.div(me, group)
    loads = []
    for d, piece in enumerate(pieces):
        start = jnp.bitwise_xor(place, d) * rows
        loads.append(pltpu.make_async_copy(piece, held.at[pl.ds(start, rows)], load_sem.at[d]))
        loads[-1].start()
    lists_load.wait()
    for load in loads:
        load.wait()

    def one_index(q, carry):
        found = []
        for x in range(boxes):
            columns = [lists_ref[q, 0, x * slots + bas * own + j] - bas * span for j in range(own)]
            for t in range(own):
                row = lists_ref[q, 0, x * slots + home * own + t] - home * group * rows
                found.append([held[row, columns[j]] for j in range(own)])
        for i, parts in enumerate(found):
            stage[q, i] = jnp.concatenate(parts, axis=1)
        pltpu.make_async_copy(stage.at[q], out_ref.at[q], sem).start()
        return carry

    lax.fori_loop(0, lists_ref.shape[0], one_index, 0, unroll=8)
    pltpu.make_async_copy(stage, out_ref, sem).wait()


def sum_kernel(parts_ref, out_ref):
    per_device = out_ref.shape[1]
    total = jnp.sum(parts_ref[...], axis=0, keepdims=True)
    for d in range(3):
        out_ref[d : d + 1, :] = total[:, d * per_device : (d + 1) * per_device]


def in_hbm(array):
    return pltpu.with_memory_space_constraint(array, pltpu.HBM)


def spread_rows(values, places):
    inside = lax.broadcasted_iota(jnp.int32, (16, 1), 0).astype(jnp.float32) == places
    uppers, rests = [], []
    for value in values:
        upper = value.astype(jnp.bfloat16).astype(jnp.float32)
        uppers.append(jnp.where(inside, upper, 0.0))
        rests.append(jnp.where(inside, value - upper, 0.0))
    return jnp.concatenate(uppers + rests, axis=0).astype(jnp.bfloat16)


def owner_rows(owners, devices):
    line = lax.broadcasted_iota(jnp.int32, (devices, 1), 0).astype(jnp.float32).astype(jnp.bfloat16)
    one = jnp.ones((), jnp.bfloat16)
    zero = jnp.zeros((), jnp.bfloat16)
    return jnp.where(line == owners.astype(jnp.bfloat16), one, zero)


def along_lanes(left, right):
    return lax.dot_general(left, right, (((1,), (1,)), ((), ())), preferred_element_type=jnp.float32)


def main_kernel(
    screen_hbm,
    chi_ref,
    dchi_ref,
    arrived_ref,
    weight_ref,
    atom_ref,
    packed_ref,
    out_ref,
    chi_buf,
    block_buf,
    packed_buf,
    turn,
    screen_ref,
    screen_sem,
    chi_sem,
    block_sem,
    packed_sem,
    *,
    per_device,
    knbr,
):
    boxes = chi_buf.shape[0]
    span, block = atom_ref.shape
    own = dchi_ref.shape[-1] // block
    bas = lax.axis_index("bas")
    n_bas = lax.axis_size("bas")
    halves = n_bas // boxes
    box_points = chi_buf.shape[1]
    points = box_points // halves
    devices = out_ref.shape[0]

    packed_copy = pltpu.make_async_copy(
        packed_ref, packed_buf, packed_sem
    )
    screen_copy = pltpu.make_async_copy(screen_hbm, screen_ref, screen_sem)
    screen_copy.start()

    def block_copies(x):
        for t in range(own):
            pltpu.make_async_copy(
                arrived_ref.at[:, :, x * own + t], block_buf.at[x, :, t], block_sem.at[x]
            ).start()

    def chi_copy(x):
        return pltpu.make_async_copy(chi_ref.at[x], chi_buf.at[x], chi_sem.at[x])

    for x in range(2):
        chi_copy(x).start()
        block_copies(x)
    packed_copy.start()
    screen_copy.wait()
    columns = [[screen_ref[x, bas * own + j] - bas * span for j in range(own)] for x in range(boxes)]

    owner_lane = lax.broadcasted_iota(jnp.int32, (1, devices), 1).astype(jnp.float32).astype(jnp.bfloat16)
    one = jnp.ones((), jnp.bfloat16)
    zero = jnp.zeros((), jnp.bfloat16)
    total = jnp.zeros((96, devices), jnp.float32)
    width = own * block
    for x in range(boxes):
        chi_copy(x).wait()
        pltpu.make_async_copy(block_buf.at[x], block_buf.at[x], block_sem.at[x]).wait()
        blocks = block_buf[x].reshape(chi_buf.shape[2], own * block)
        fock = jnp.dot(chi_buf[x], blocks, preferred_element_type=jnp.float32)
        if x + 2 < boxes:
            chi_copy(x + 2).start()
            block_copies(x + 2)
        own_chi = chi_buf[x, :, pl.ds(pl.multiple_of(bas * width, width), width)]
        energy = jnp.sum(own_chi.astype(jnp.float32) * fock, axis=1, keepdims=True)
        weighted = fock * (-2.0 * weight_ref[:, x : x + 1])
        terms = [
            jnp.sum(dchi_ref[d, x].astype(jnp.float32) * weighted, axis=0, keepdims=True)
            for d in range(3)
        ]
        atoms = jnp.concatenate(
            [
                atom_ref[pl.ds(columns[x][j], 1), :]
                for j in range(own)
            ],
            axis=1,
        )
        owners = lax.div(atoms, per_device)
        inside = (atoms - owners * per_device).astype(jnp.float32)
        total += along_lanes(
            spread_rows(terms, inside), owner_rows(owners.astype(jnp.float32), devices)
        )
        if x == 0:
            packed_copy.wait()
        for h in range(halves):
            at = x * halves + h
            turn[:points, :] = jnp.broadcast_to(energy[h * points : (h + 1) * points], (points, 128))
            energy_row = turn[...].T[0:1, :]
            energy_row = jnp.where(
                lax.broadcasted_iota(jnp.int32, energy_row.shape, 1) < points, energy_row, 0.0
            )

            def lanes(c, at=at):
                return jnp.concatenate(
                    [packed_buf[at, (c * 2 + p) * knbr : (c * 2 + p + 1) * knbr, :] for p in range(2)],
                    axis=1,
                )

            grads = [lanes(d) * energy_row for d in range(3)]
            places = lanes(3)
            owners = packed_buf[at, 8 * knbr : 8 * knbr + 256, :].astype(jnp.bfloat16)
            left = jnp.concatenate(
                [
                    spread_rows([g[k : k + 1] for g in grads], places[k : k + 1])
                    for k in range(knbr)
                ],
                axis=1,
            )
            right = jnp.concatenate(
                [
                    jnp.where(owner_lane == owners[:, k : k + 1], one, zero)
                    for k in range(knbr)
                ],
                axis=0,
            )
            total += jnp.dot(left, right, preferred_element_type=jnp.float32)
    both = total[:48] + total[48:]
    parts = [both[d * 16 : d * 16 + per_device] for d in range(3)]
    parts.append(jnp.zeros((128 - 3 * per_device, devices), jnp.float32))
    out_ref[...] = jnp.concatenate(parts, axis=0).T


def run_main(screen, chi, dchi, arrived, weight_lines, atoms, gathered, devices, per_device):
    boxes = chi.shape[0]
    n_bas = lax.axis_size("bas")
    knbr = 8
    hbm = pl.BlockSpec(memory_space=pltpu.HBM)
    vmem = pl.BlockSpec(memory_space=pltpu.VMEM)
    ranges, group, asked, part, width = arrived.shape
    return pl.pallas_call(
        functools.partial(main_kernel, per_device=per_device, knbr=knbr),
        out_shape=jax.ShapeDtypeStruct((devices, 128), jnp.float32),
        in_specs=[hbm, hbm, vmem, hbm, vmem, vmem, hbm],
        out_specs=vmem,
        scratch_shapes=[
            pltpu.VMEM(chi.shape, chi.dtype),
            pltpu.VMEM((boxes, ranges, asked // boxes, group, part, width), arrived.dtype),
            pltpu.VMEM((n_bas, 8 * knbr + 256, 128), jnp.float32),
            pltpu.VMEM((256, 128), jnp.float32),
            pltpu.SMEM(screen.shape, jnp.int32),
            pltpu.SemaphoreType.DMA,
            pltpu.SemaphoreType.DMA((boxes,)),
            pltpu.SemaphoreType.DMA((boxes,)),
            pltpu.SemaphoreType.DMA,
        ],
        compiler_params=pltpu.CompilerParams(vmem_limit_bytes=28 * MIB),
        cost_estimate=pl.CostEstimate(flops=2_000_000_000, bytes_accessed=30_000_000, transcendentals=0),
    )(
        screen,
        chi,
        dchi,
        arrived,
        weight_lines,
        atoms,
        gathered,
    )


def shards(chi, dchi, screen, density, weights, basis_atom, neighbors, weight_grad):
    boxes, points, _ = chi.shape
    rows, span, block, _ = density.shape
    n_pts = lax.axis_size("pts")
    n_bas = lax.axis_size("bas")
    devices = n_pts * n_bas
    slots = screen.shape[1]
    own = slots // n_bas
    knbr = neighbors.shape[0]
    per_device = 12
    hbm = pl.BlockSpec(memory_space=pltpu.HBM)
    vmem = pl.BlockSpec(memory_space=pltpu.VMEM)

    group = n_pts // n_bas
    *pieces, packed, flat = pl.pallas_call(
        functools.partial(first_kernel, group=group),
        out_shape=[pltpu.HBM((rows, span, block // group, block), density.dtype)] * group
        + [
            jax.ShapeDtypeStruct((8 * knbr, 128), jnp.float32),
            jax.ShapeDtypeStruct((n_pts, 1, boxes * slots), jnp.int32),
        ],
        in_specs=[hbm] * 4,
        out_specs=[hbm] * group + [vmem] * 2,
        scratch_shapes=[
            pltpu.VMEM(density.shape, density.dtype),
            pltpu.VMEM(weight_grad.shape, jnp.float32),
            pltpu.VMEM(neighbors.shape, jnp.int32),
            pltpu.VMEM(screen.shape, jnp.int32),
            pltpu.VMEM((4, knbr, 256), jnp.float32),
            pltpu.SemaphoreType.DMA((rows,)),
            pltpu.SemaphoreType.DMA((group, rows)),
            pltpu.SemaphoreType.DMA((3,)),
        ],
        compiler_params=pltpu.CompilerParams(vmem_limit_bytes=12 * MIB),
    )(in_hbm(density), in_hbm(screen), in_hbm(weight_grad), in_hbm(neighbors))
    pieces = [in_hbm(pieces[0])] + [
        lax.ppermute(pieces[d], "pts", [(p, p ^ d) for p in range(n_pts)]) for d in range(1, group)
    ]
    lists = lax.all_to_all(flat, "pts", split_axis=0, concat_axis=0, tiled=True)
    unpacked, weight_lines = pl.pallas_call(
        functools.partial(unpack_kernel, per_device=per_device, knbr=knbr),
        out_shape=(
            jax.ShapeDtypeStruct((n_bas, 8 * knbr + 256, 128), jnp.float32),
            jax.ShapeDtypeStruct((points, 128), jnp.float32),
        ),
        in_specs=[vmem] * 2,
        out_specs=(vmem, vmem),
        scratch_shapes=[
            pltpu.VMEM((n_bas, 128, 256), jnp.float32),
            pltpu.VMEM((128, 512), jnp.float32),
        ],
        compiler_params=pltpu.CompilerParams(vmem_limit_bytes=12 * MIB),
        cost_estimate=pl.CostEstimate(flops=5_000_000, bytes_accessed=4_000_000, transcendentals=0),
    )(lax.all_gather(packed, "bas", axis=0), weights)
    outgoing = pl.pallas_call(
        functools.partial(send_kernel, boxes=boxes, slots=slots, own=own),
        out_shape=pltpu.HBM((n_pts, boxes * own, block // group, own * block), density.dtype),
        in_specs=[hbm] * (group + 1),
        out_specs=hbm,
        scratch_shapes=[
            pltpu.SMEM(lists.shape, jnp.int32),
            pltpu.VMEM((group * rows, span, block // group, block), density.dtype),
            pltpu.VMEM((n_pts, boxes * own, block // group, own * block), density.dtype),
            pltpu.SemaphoreType.DMA,
            pltpu.SemaphoreType.DMA((group,)),
            pltpu.SemaphoreType.DMA,
        ],
        compiler_params=pltpu.CompilerParams(vmem_limit_bytes=12 * MIB),
    )(lists, *pieces)
    arrived = lax.all_to_all(outgoing, "pts", split_axis=0, concat_axis=0, tiled=True)
    arrived = arrived.reshape(n_bas, group, boxes * own, block // group, own * block)

    parts = run_main(
        in_hbm(screen),
        in_hbm(chi),
        dchi,
        in_hbm(arrived),
        weight_lines,
        basis_atom.reshape(span, block),
        in_hbm(unpacked),
        devices,
        per_device,
    )
    parts = parts[:, : 3 * per_device].reshape(devices, 1, 3 * per_device)
    parts = lax.all_to_all(parts, ("pts", "bas"), split_axis=0, concat_axis=0, tiled=True)
    return pl.pallas_call(
        sum_kernel,
        out_shape=jax.ShapeDtypeStruct((3, per_device), jnp.float32),
        in_specs=[vmem],
        out_specs=vmem,
        compiler_params=pltpu.CompilerParams(vmem_limit_bytes=4 * MIB),
    )(parts.reshape(devices, 3 * per_device))


def solution(mesh):
    in_specs = (
        P("pts", None, None),
        P(None, "pts", None, "bas"),
        P("pts", None),
        P("pts", "bas", None, None),
        P("pts", None),
        P("bas"),
        P(None, ("pts", "bas")),
        P(None, None, ("pts", "bas")),
    )
    out_specs = P(None, ("pts", "bas"))
    return jax.shard_map(shards, mesh=mesh, in_specs=in_specs, out_specs=out_specs, check_vma=False)
```
